256 devices in a mesh: inner: 8 (over y, z_hi), outer: 32 (over z_lo, x, core).
Axes of the slice: x: 4, y: 4, z: 8 (z_hi: 2, z_lo: 4; z = z_hi * 4 + z_lo), core: 2. Of those that a mesh axis runs over, the one named last changes fastest.
Arguments:
- queries: bfloat16 [2, 32, 8, 64, 4, 128], P(None, 'outer', 'inner'), may hold values from -20 to 20
- key_maps: bfloat16 [2, 32, 8, 64, 128], P(None, 'outer', 'inner'), may hold values from -20 to 20
- values: bfloat16 [2, 32, 8, 64, 128], P(None, 'outer', 'inner'), may hold values from -6 to 6
- lambdas: float32 [4], replicated, may hold values from 0.2 to 0.7
- norm_gain: float32 [128], replicated, may hold values from 0.1 to 1.9
- out_grad: bfloat16 [2, 32, 8, 64, 4, 128], P(None, 'outer', 'inner'), may hold values from -6 to 6
Outputs:
- attended: bfloat16 [2, 32, 8, 64, 4, 128], P(None, 'outer', 'inner')
- query_grad: bfloat16 [2, 32, 8, 64, 4, 128], P(None, 'outer', 'inner')
The draws below stay inside these ranges and needn't reach their ends.
All inputs are finite; a program needn't handle non-finite values.
Results may differ from the reference program's by a relative error of at most 0.024.
Values may be sent and summed in bfloat16 or wider, within the bound.
A program may use at most 128 MiB of HBM per device.

```python
import math
import jax
import jax.numpy as jnp
from jax import lax

HALF = 64
QH = 4
DK = 64
DV = 128
TOKENS = 32768
N_INNER = 8
N_OUTER = 32


def draw_key_maps(key, part):
    key = jax.random.fold_in(key, 3)
    first_key = jax.random.fold_in(key, 0)
    array_shape = (2, N_OUTER, N_INNER, HALF, 2 * DK)
    result = jnp.clip(jax.random.normal(first_key, array_shape, jnp.float32), -6.0, 6.0)
    return result.astype(jnp.bfloat16)


def draw_queries(key, part):
    key = jax.random.fold_in(key, 5)
    first_key = jax.random.fold_in(key, 0)
    array_shape = (2, N_OUTER, N_INNER, HALF, QH, 2 * DK)
    result = jnp.clip(jax.random.normal(first_key, array_shape, jnp.float32), -6.0, 6.0)
    return result.astype(jnp.bfloat16)


def level_of(own_key, shape, pieces, least, largest):
    def one(position, parts):
        steps = jax.random.uniform(jax.random.fold_in(jax.random.fold_in(own_key, 6), position), (parts,), jnp.float32, least / len(pieces), largest / len(pieces))
        return jnp.repeat(jnp.exp(steps), shape[position] // parts).reshape((-1,) + (1,) * (len(shape) - position - 1))

    gain = one(*pieces[0])
    for cut in pieces[1:]:
        gain = gain * one(*cut)
    return gain


def centred(stream_key, dims, width, most, cuts=(), kind=jnp.bfloat16):
    array = width * jax.random.normal(stream_key, dims, jnp.float32)
    if cuts:
        array = array * level_of(stream_key, dims, cuts, -0.22, 0.18)
    return jnp.clip(array, -most, most).astype(kind)


def setup_inputs(seed: int = 0) -> dict:
    splits = jax.random.split(jax.random.key(seed), 7)
    queries = draw_queries(jax.random.fold_in(splits[6], 71), 0)
    key_maps = draw_key_maps(jax.random.fold_in(splits[6], 71), 0)
    values = centred(splits[2], (2, N_OUTER, N_INNER, HALF, DV), 1.0, 6.0, ((1, 32), (2, 8)))
    lambdas = jnp.clip(jax.random.uniform(splits[3], (QH,), jnp.float32, 0.2, 0.7), 0.2, 0.7)
    norm_gain = jnp.clip(1.0 + 0.18 * jax.random.normal(splits[4], (DV,), jnp.float32), 0.1, 1.9)
    out_grad = centred(splits[5], (2, N_OUTER, N_INNER, HALF, QH, DV), 1.0, 6.0, ((1, 32), (2, 8)))
    return dict(queries=queries, key_maps=key_maps, values=values, lambdas=lambdas, norm_gain=norm_gain, out_grad=out_grad)


lam_init = 0.8 - 0.6 * math.exp(-3.3)
norm_eps = 1e-05
far_below = -1e+30

def contract(left_op, right_op):
    return lax.dot_general(left_op, right_op, (((1,), (1,)), ((), ())), preferred_element_type=jnp.float32)

def absorb(run_top, run_sum, run_acc, scores, visible, vblock):
    new_top = jnp.maximum(run_top, lax.optimization_barrier(jnp.max(jnp.where(visible, scores, far_below), axis=1)))
    weights = jnp.exp(jnp.where(visible, scores - new_top[:, None], far_below))
    shrink = jnp.exp(run_top - new_top)
    run_sum = run_sum * shrink + lax.optimization_barrier(jnp.sum(weights, axis=1))
    run_acc = run_acc * shrink[:, None] + jnp.dot(weights.astype(jnp.bfloat16), vblock, preferred_element_type=jnp.float32)
    return (new_top, run_sum, run_acc)

def forward_block(running, qblock, query_pos, kblock, vblock, key_pos, score_scale):
    map_width = kblock.shape[1] // 2
    visible = key_pos[None, :] <= query_pos[:, None]
    first_map = contract(qblock[:, :map_width], kblock[:, :map_width]) * score_scale
    second_map = contract(qblock[:, map_width:], kblock[:, map_width:]) * score_scale
    part_one = absorb(running[0], running[1], running[2], first_map, visible, vblock)
    part_two = absorb(running[3], running[4], running[5], second_map, visible, vblock)
    return part_one + part_two

def finish_forward(running, lambdas, norm_gain, grad_block, out_scale):
    top_one, sum_one, acc_one, top_two, sum_two, acc_two = running
    row_count = sum_one.shape[0]
    head_count = lambdas.shape[0]
    tok_count = row_count // head_count
    vwidth = acc_one.shape[1]
    out_one = (acc_one / sum_one[:, None]).reshape(tok_count, head_count, vwidth)
    out_two = (acc_two / sum_two[:, None]).reshape(tok_count, head_count, vwidth)
    lam_col = lambdas[None, :, None]
    differ = out_one - lam_col * out_two
    inv_rms = lax.rsqrt(lax.optimization_barrier(jnp.mean(differ * differ, axis=-1, keepdims=True)) + norm_eps)
    attended = (out_scale * norm_gain * differ * inv_rms).astype(jnp.bfloat16)
    scaled_grad = grad_block.astype(jnp.float32) * (out_scale * norm_gain)
    d_differ = inv_rms * scaled_grad - differ * inv_rms ** 3 * lax.optimization_barrier(jnp.mean(scaled_grad * differ, axis=-1, keepdims=True))
    dot_one = lax.optimization_barrier(jnp.sum(d_differ * out_one, axis=-1)).reshape(row_count)
    dot_two = lax.optimization_barrier(jnp.sum(d_differ * out_two, axis=-1)).reshape(row_count)
    lse_one = top_one + jnp.log(sum_one)
    lse_two = top_two + jnp.log(sum_two)
    lam_rows = jnp.tile(lambdas, tok_count)
    back_rows = d_differ.reshape(row_count, vwidth).astype(jnp.bfloat16)
    return (attended, (lse_one, lse_two, dot_one, dot_two, lam_rows, back_rows))

def backward_block(grad_pair, qblock, query_pos, kblock, vblock, key_pos, score_scale, saved_stats):
    lse_one, lse_two, dot_one, dot_two, lam_rows, back_rows = saved_stats
    map_width = kblock.shape[1] // 2
    visible = key_pos[None, :] <= query_pos[:, None]
    first_map = contract(qblock[:, :map_width], kblock[:, :map_width]) * score_scale
    second_map = contract(qblock[:, map_width:], kblock[:, map_width:]) * score_scale
    prob_one = jnp.exp(jnp.where(visible, first_map - lse_one[:, None], far_below))
    prob_two = jnp.exp(jnp.where(visible, second_map - lse_two[:, None], far_below))
    through = contract(back_rows, vblock)
    slope_one = (prob_one * (through - dot_one[:, None])).astype(jnp.bfloat16)
    slope_two = (-lam_rows[:, None] * prob_two * (through - dot_two[:, None])).astype(jnp.bfloat16)
    grad_one = grad_pair[0] + jnp.dot(slope_one, kblock[:, :map_width], preferred_element_type=jnp.float32)
    grad_two = grad_pair[1] + jnp.dot(slope_two, kblock[:, map_width:], preferred_element_type=jnp.float32)
    return (grad_one, grad_two)

def sort_tokens(source):
    tail_dims = source.shape[4:]
    blocks = N_OUTER * N_INNER
    lower_half = source[0].reshape((blocks * HALF,) + tail_dims)
    upper_half = source[1].reshape((blocks, HALF) + tail_dims)[::-1]
    return jnp.concatenate([lower_half, upper_half.reshape((blocks * HALF,) + tail_dims)], axis=0)

def unsort_tokens(source):
    tail_dims = source.shape[1:]
    blocks = N_OUTER * N_INNER
    lower_half = source[:blocks * HALF].reshape((N_OUTER, N_INNER, HALF) + tail_dims)
    upper_half = source[blocks * HALF:].reshape((blocks, HALF) + tail_dims)[::-1]
    return jnp.stack([lower_half, upper_half.reshape((N_OUTER, N_INNER, HALF) + tail_dims)], axis=0)

def reference(queries, key_maps, values, lambdas, norm_gain, out_grad):
    score_scale = 1.0 / math.sqrt(DK)
    out_scale = 1.0 - lam_init
    query_rows = sort_tokens(queries)
    key_rows = sort_tokens(key_maps)
    value_rows = sort_tokens(values)
    grad_rows = sort_tokens(out_grad)
    block_len = min(512, TOKENS)
    row_count = block_len * QH
    empty_state = (jnp.full((row_count,), far_below, jnp.float32), jnp.zeros((row_count,), jnp.float32), jnp.zeros((row_count, DV), jnp.float32)) * 2
    zero_grads = (jnp.zeros((row_count, DK), jnp.float32),) * 2

    def tile_keys(tile_id):
        start_at = tile_id * block_len
        kblock = lax.dynamic_slice_in_dim(key_rows, start_at, block_len, 0)
        vblock = lax.dynamic_slice_in_dim(value_rows, start_at, block_len, 0)
        key_pos = start_at + jnp.arange(block_len, dtype=jnp.int32)
        return (kblock, vblock, key_pos)

    def one_block(block_id):
        start_at = block_id * block_len
        qblock = lax.dynamic_slice_in_dim(query_rows, start_at, block_len, 0).reshape(row_count, 2 * DK)
        query_pos = start_at + jnp.arange(row_count, dtype=jnp.int32) // QH
        first_tile = jnp.zeros((), jnp.int32)

        def forward_turn(tile_id, running):
            kblock, vblock, key_pos = tile_keys(tile_id)
            return forward_block(running, qblock, query_pos, kblock, vblock, key_pos, score_scale)
        running = lax.fori_loop(first_tile, block_id + 1, forward_turn, empty_state)
        grads_here = lax.dynamic_slice_in_dim(grad_rows, start_at, block_len, 0)
        attended, saved_stats = finish_forward(running, lambdas, norm_gain, grads_here, out_scale)

        def backward_turn(tile_id, grad_pair):
            kblock, vblock, key_pos = tile_keys(tile_id)
            return backward_block(grad_pair, qblock, query_pos, kblock, vblock, key_pos, score_scale, saved_stats)
        grad_pair = lax.fori_loop(first_tile, block_id + 1, backward_turn, zero_grads)
        query_grad = (jnp.concatenate(grad_pair, axis=1) * score_scale).astype(jnp.bfloat16)
        return (attended, query_grad.reshape(block_len, QH, 2 * DK))
    results = lax.map(one_block, jnp.arange(TOKENS // block_len, dtype=jnp.int32))
    attended = unsort_tokens(results[0].reshape(TOKENS, QH, DV))
    query_grad = unsort_tokens(results[1].reshape(TOKENS, QH, 2 * DK))
    return (attended, query_grad)
```

```python
import math

import jax
import jax.numpy as jnp
from jax import lax
from jax.experimental import pallas as pl
from jax.experimental.pallas import tpu as pltpu
from jax.sharding import PartitionSpec as P

lam_init = 0.8 - 0.6 * math.exp(-3.3)
OUT = 1.0 - lam_init
EPS = 1e-5
NEG = -1e30
F32, BF = jnp.float32, jnp.bfloat16
R = 256
CH = 512
MESH = pl.DeviceIdType.MESH


def nt(a, b):
    return lax.dot_general(a, b, (((1,), (1,)), ((), ())), preferred_element_type=F32)


def tn(a, b):
    return lax.dot_general(a, b, (((0,), (0,)), ((), ())), preferred_element_type=F32)


def device_at(x, y, z, core):
    return (y * 2 + z // 4, ((z % 4) * 4 + x) * 2 + core)


def kernel(
    q_ref, k_ref, v_ref, lam_ref, gain_ref, og_ref, att_ref, qg_ref,
    kv, w, qm, top, tot, acc, tops, back, dots, grads,
    zs, zr, s1, r1, s2, r2, ss, sr,
):
    inner, outer = lax.axis_index("inner"), lax.axis_index("outer")
    y, z = inner // 2, (inner % 2) * 4 + outer // 8
    x, core = (outer // 2) % 4, outer % 2
    first = core == 0
    a_pos, b_pos = jnp.where(first, x, y), jnp.where(first, y, x)

    def place(a, b):
        return jnp.where(first, a, b), jnp.where(first, b, a)

    def plane_device(da, db):
        px, py = place((a_pos + da) % 4, (b_pos + db) % 4)
        return device_at(px, py, z, core)

    up, down = device_at(x, y, (z + 1) % 8, core), device_at(x, y, (z + 7) % 8, core)
    sibling = device_at(x, y, z, 1 - core)

    def unit_z(k):
        half = (k + 1) // 2
        return (z + jnp.where(k % 2 == 1, half, 8 - half)) % 8

    def piece(k, da, db):
        px, py = place((a_pos + da) % 4, (b_pos + db) % 4)
        return kv.at[unit_z(k), px, core, py]

    def send(ref, send_sem, recv_sem, device):
        return pltpu.make_async_remote_copy(
            src_ref=ref, dst_ref=ref, send_sem=send_sem, recv_sem=recv_sem,
            device_id=device, device_id_type=MESH,
        )

    def z_copy(k, unit, device):
        return send(piece(k, 0, 0), zs.at[unit], zr.at[unit], device)

    def one_copy(k, slot):
        sign = 1 - 2 * (k % 2)
        if slot == 2:
            return send(piece(k, 4 - sign, 0), s1.at[k, 2], r1.at[k, 2], plane_device(4 + sign, 0))
        return send(piece(k, 0, 0), s1.at[k, slot], r1.at[k, slot], plane_device((1, 3)[slot], 0))

    def one_wait(k, slot):
        send(piece(k, (3, 1, 2)[slot], 0), s1.at[k, slot], r1.at[k, slot], sibling).wait_recv()

    SIDE = (0, 3, 1, 2)

    def two_copy(k, m, slot):
        if slot == 2:
            sign = (1, 3)[m % 2]
            return send(piece(k, SIDE[m], 4 - sign), s2.at[k, m, 2], r2.at[k, m, 2], plane_device(0, sign))
        return send(piece(k, SIDE[m], 0), s2.at[k, m, slot], r2.at[k, m, slot], plane_device(0, (1, 3)[slot]))

    def two_wait(k, m, slot):
        send(piece(k, SIDE[m], (3, 1, 2)[slot]), s2.at[k, m, slot], r2.at[k, m, slot], sibling).wait_recv()

    def pair_copy(k, mine):
        ref = kv.at[unit_z(k), :, core if mine else 1 - core]
        return send(ref, ss.at[k], sr.at[k], sibling)

    for c in range(2):
        kv[z, x, core, y, c, 0] = k_ref[c]
        kv[z, x, core, y, c, 1] = v_ref[c]
    barrier = pltpu.get_barrier_semaphore()
    for device in (up, down, sibling, plane_device(1, 0), plane_device(3, 0), plane_device(0, 1), plane_device(0, 3)):
        pl.semaphore_signal(barrier, inc=1, device_id=device, device_id_type=MESH)
    pl.semaphore_wait(barrier, 7)
    z_copy(0, 1, down).start()
    z_copy(0, 2, up).start()

    lane = lax.broadcasted_iota(jnp.int32, (R, 128), 1)
    for c in range(2):
        qv = q_ref[c] * jnp.asarray(0.125, BF)
        zero = jnp.zeros_like(qv)
        qm[c, :R] = jnp.where(lane < 64, qv, zero)
        qm[c, R:] = jnp.where(lane < 64, zero, qv)
    top[...] = jnp.full_like(top, NEG)
    acc[...] = jnp.zeros_like(acc)
    tot[...] = jnp.zeros_like(tot)

    def stage_first(k):
        @pl.when(k > 0)
        def _():
            send(piece(k, 0, 0), zs.at[k], zr.at[k], sibling).wait_recv()

            @pl.when((k % 2 == 1) & (k + 2 <= 7))
            def _():
                z_copy(k, k + 2, down).start()

            @pl.when((k % 2 == 0) & (k + 2 <= 6))
            def _():
                z_copy(k, k + 2, up).start()

        one_copy(k, 0).start()
        one_copy(k, 1).start()

    def stage_first_on(k):
        one_wait(k, 0)
        one_wait(k, 1)
        one_copy(k, 2).start()

    def stage_second(k):
        one_wait(k, 2)
        for m in range(4):
            two_copy(k, m, 0).start()
            two_copy(k, m, 1).start()

    def stage_second_on(k, m):
        two_wait(k, m, 0)
        two_wait(k, m, 1)
        two_copy(k, m, 2).start()

    def stage_pair(k):
        for m in range(4):
            two_wait(k, m, 2)
        pair_copy(k, True).start()

    def stage_ready(k):
        pair_copy(k, False).wait_recv()

    def keys_of(zz, xx, c):
        return (
            kv[zz, xx, :, :, c, 0].reshape(CH, 128),
            kv[zz, xx, :, :, c, 1].reshape(CH, 128),
        )

    def tasks(specs):
        loaded = []
        for tid, st, cq, ck, zz, xx, mask in specs:
            loaded.append((*keys_of(zz, xx, ck), qm[cq], top[st], tot[st], acc[st]))
        out = []
        for spec, (kb, vb, qq, old, total, a) in zip(specs, loaded):
            s = nt(kb, qq)
            if spec[-1] is not None:
                s = jnp.where(jnp.concatenate([spec[-1]] * 2, axis=1), s, NEG)
            new = jnp.maximum(old, jnp.max(s, axis=0, keepdims=True))
            p = jnp.exp(s - new)
            shrink = jnp.exp(old - new)
            total = total * shrink + jnp.sum(p, axis=0, keepdims=True)
            p = p.astype(BF)
            out.append((p, new, total, a * shrink + tn(vb, p)))
        for (tid, st, *_), (p, new, total, a) in zip(specs, out):
            w[tid] = p
            top[st] = new
            tot[st] = total
            acc[st] = a
            tops[tid] = new

    mine = core * 8 + inner

    def forward(k, h):
        zz, xx = unit_z(k), (x + 1 + h) % 4
        tid = 2 * (4 * k + h)
        own = ((zz * 4 + xx) % 16) * 2 + core
        here = ((z * 4 + x) % 16) * 2 + core
        c = jnp.where(own > here, 1, 0)
        if h < 3:
            tasks([(tid, 2, 1, 0, zz, xx, None), (tid + 1, c, c, c, zz, xx, None)])
            return
        edge = (k == 0) | (k == 7)

        @pl.when(jnp.logical_not(edge))
        def _():
            tasks([(tid, 2, 1, 0, zz, xx, None), (tid + 1, c, c, c, zz, xx, None)])

        @pl.when(edge)
        def _():
            key = lax.broadcasted_iota(jnp.int32, (CH, R), 0)
            tok = lax.broadcasted_iota(jnp.int32, (CH, R), 1) // 4
            blk = (key // 256) * 8 + ((key // 64) % 4) * 2 + zz // 4
            diag = (blk == mine) & (key % 64 <= tok)
            tasks([(tid, 2, 1, 0, zz, xx, None)])
            tasks([(tid + 1, 0, 0, 0, zz, xx, (blk < mine) | diag)])
            tasks([(64 + k // 7, 1, 1, 1, zz, xx, (blk > mine) | diag)])

    def gated(fn, k, *args):
        @pl.when((k >= 0) & (k < 8))
        def _():
            fn(k, *args)

    def turn(g, carry):
        gated(stage_first, g)
        gated(stage_second, g - 1)
        gated(stage_ready, g - 3)
        gated(forward, g - 3, 0)
        gated(forward, g - 3, 1)
        gated(stage_pair, g - 2)
        gated(stage_first_on, g)
        gated(stage_second_on, g - 1, 0)
        gated(stage_second_on, g - 1, 1)
        gated(forward, g - 3, 2)
        gated(stage_second_on, g - 1, 2)
        gated(stage_second_on, g - 1, 3)
        gated(forward, g - 3, 3)
        return carry

    lax.fori_loop(0, 11, turn, 0)

    head = lax.broadcasted_iota(jnp.int32, (1, R), 1) % 4
    lam = jnp.where(
        head == 0, lam_ref[0], jnp.where(head == 1, lam_ref[1], jnp.where(head == 2, lam_ref[2], lam_ref[3]))
    )
    gain = jnp.transpose(jnp.broadcast_to(gain_ref[...] * OUT, (R, 128)))
    for c in range(2):
        a, m, total = acc[c], top[c], tot[c]
        if c == 1:
            m2 = top[2]
            mm = jnp.maximum(m, m2)
            e1, e2 = jnp.exp(m - mm), jnp.exp(m2 - mm)
            a = a * e1 + acc[2] * e2
            total = total * e1 + tot[2] * e2
            m = mm
        a = a / total
        outs = [a[:, :R], a[:, R:]]
        lse = m + jnp.log(total)
        top[c] = lse
        if c == 1:
            top[2] = lse
        differ = outs[0] - lam * outs[1]
        inv = lax.rsqrt(jnp.mean(differ * differ, axis=0, keepdims=True) + EPS)
        att_ref[c] = jnp.transpose(gain * differ * inv).astype(BF)
        scaled = jnp.transpose(og_ref[c].astype(F32)) * gain
        dd = inv * scaled - differ * (inv * inv * inv) * jnp.mean(scaled * differ, axis=0, keepdims=True)
        for j in range(2):
            dots[c, :, j * R:j * R + R] = jnp.sum(dd * outs[j], axis=0, keepdims=True)
        back[c] = jnp.transpose(dd).astype(BF)

    grads[...] = jnp.zeros_like(grads)

    def back_tasks(specs):
        loaded = []
        for tid, st, cq, ck, zz, xx in specs:
            loaded.append((*keys_of(zz, xx, ck), back[cq], dots[cq], w[tid], tops[tid], top[st], grads[st]))
        out = []
        for kb, vb, bk, d, p, tp, lse, g in loaded:
            t = nt(vb, bk)
            slope = p * (jnp.concatenate([t, t], axis=1) - d).astype(BF)
            both = jnp.concatenate([tn(kb[:, :64], slope[:, :R]), tn(kb[:, 64:], slope[:, R:])], axis=1)
            out.append(g + both * jnp.exp(tp - lse))
        for spec, g in zip(specs, out):
            grads[spec[1]] = g

    def backward(n, carry):
        k, h = n // 4, n % 4
        zz, xx = unit_z(k), (x + 1 + h) % 4
        c = jnp.where((zz * 4 + xx) % 16 > (z * 4 + x) % 16, 1, 0)
        back_tasks([(2 * n, 2, 1, 0, zz, xx), (2 * n + 1, c, c, c, zz, xx)])
        return carry

    lax.fori_loop(0, 32, backward, 0)
    back_tasks([(64, 1, 1, 1, z, x)])
    back_tasks([(65, 1, 1, 1, (z + 4) % 8, x)])
    for c in range(2):
        g1, g2 = grads[c, :, :R], grads[c, :, R:]
        if c == 1:
            g1, g2 = g1 + grads[2, :, :R], g2 + grads[2, :, R:]
        qg_ref[c] = (0.125 * jnp.transpose(jnp.concatenate([g1, -lam * g2], axis=0))).astype(BF)

    def drain(k, carry):
        @pl.when(k > 0)
        def _():
            send(piece(k, 0, 0), zs.at[k], zr.at[k], sibling).wait_send()

        for slot in range(3):
            one_copy(k, slot).wait_send()
            for m in range(4):
                two_copy(k, m, slot).wait_send()
        pair_copy(k, True).wait_send()
        return carry

    lax.fori_loop(0, 8, drain, 0)


def body(queries, key_maps, values, lambdas, norm_gain, out_grad):
    V = pl.BlockSpec(memory_space=pltpu.VMEM)
    S = pl.BlockSpec(memory_space=pltpu.SMEM)
    dma = pltpu.SemaphoreType.DMA
    att, qg = pl.pallas_call(
        kernel,
        out_shape=(jax.ShapeDtypeStruct((2, R, 128), BF),) * 2,
        in_specs=[V, V, V, S, V, V],
        out_specs=(V, V),
        scratch_shapes=[
            pltpu.VMEM((8, 4, 2, 4, 2, 2, 64, 128), BF),
            pltpu.VMEM((66, CH, 2 * R), BF),
            pltpu.VMEM((2, 2 * R, 128), BF),
            pltpu.VMEM((3, 1, 2 * R), F32),
            pltpu.VMEM((3, 1, 2 * R), F32),
            pltpu.VMEM((3, 128, 2 * R), F32),
            pltpu.VMEM((66, 1, 2 * R), F32),
            pltpu.VMEM((2, R, 128), BF),
            pltpu.VMEM((2, 1, 2 * R), F32),
            pltpu.VMEM((3, 64, 2 * R), F32),
            dma((8,)), dma((8,)),
            dma((8, 3)), dma((8, 3)),
            dma((8, 4, 3)), dma((8, 4, 3)),
            dma((8,)), dma((8,)),
        ],
        compiler_params=pltpu.CompilerParams(
            collective_id=0, has_side_effects=True, vmem_limit_bytes=60 * 2**20
        ),
        cost_estimate=pl.CostEstimate(flops=13 * 10**9, bytes_accessed=2**21, transcendentals=17 * 10**6),
    )(
        queries.reshape(2, R, 128),
        key_maps.reshape(2, 64, 128),
        values.reshape(2, 64, 128),
        lambdas,
        norm_gain.reshape(1, 128),
        out_grad.reshape(2, R, 128),
    )
    shape = queries.shape
    return att.reshape(shape), qg.reshape(shape)


def solution(mesh):
    wide = P(None, "outer", "inner", None, None, None)
    keys = P(None, "outer", "inner", None, None)
    return jax.shard_map(
        body, mesh=mesh, in_specs=(wide, keys, keys, P(), P(), wide), out_specs=(wide, wide), check_vma=False
    )
```

```python
import math

import jax
import jax.numpy as jnp
from jax import lax
from jax.experimental import pallas as pl
from jax.experimental.pallas import tpu as pltpu
from jax.sharding import PartitionSpec as P

lam_init = 0.8 - 0.6 * math.exp(-3.3)
OUT = 1.0 - lam_init
EPS = 1e-5
NEG = -1e30
F32, BF = jnp.float32, jnp.bfloat16
R = 256
CH = 512
MESH = pl.DeviceIdType.MESH
ORDER = ((3, 0), (6, 1), (8, 2), (10, 3), (11, 6), (12, 4), (13, 7), (14, 5))
LINES = (9, 12)


def nt(a, b):
    return lax.dot_general(a, b, (((1,), (1,)), ((), ())), preferred_element_type=F32)


def tn(a, b):
    return lax.dot_general(a, b, (((0,), (0,)), ((), ())), preferred_element_type=F32)


def device_at(x, y, z, core):
    return (y * 2 + z // 4, ((z % 4) * 4 + x) * 2 + core)


def kernel(
    q_ref, k_ref, v_ref, lam_ref, gain_ref, og_ref, att_ref, qg_ref,
    kv, w, qm, top, tot, acc, tops, back, dots, grads, sbuf, bounds,
    sent, zr, pr, r1, r2, sr,
):
    inner, outer = lax.axis_index("inner"), lax.axis_index("outer")
    y, z = inner // 2, (inner % 2) * 4 + outer // 8
    x, core = (outer // 2) % 4, outer % 2
    first = core == 0
    a_pos, b_pos = jnp.where(first, x, y), jnp.where(first, y, x)

    def place(a, b):
        return jnp.where(first, a, b), jnp.where(first, b, a)

    def plane_device(da, db):
        px, py = place((a_pos + da) % 4, (b_pos + db) % 4)
        return device_at(px, py, z, core)

    sibling = device_at(x, y, z, 1 - core)
    SIDE = (0, 3, 1, 2)

    def unit_step(k):
        half = jnp.where(k >= 6, 1, jnp.where(k == 0, 0, (k + 1) // 2 + 1))
        ahead = jnp.where(k >= 6, k == 6, k % 2 == 1)
        return jnp.where(ahead, half, 8 - half)

    def unit_z(k):
        return (z + unit_step(k)) % 8

    def piece(k, da, db):
        px, py = place((a_pos + da) % 4, (b_pos + db) % 4)
        return kv.at[unit_z(k), px, core, py]

    def send(ref, send_sem, recv_sem, device):
        return pltpu.make_async_remote_copy(
            src_ref=ref, dst_ref=ref, send_sem=send_sem, recv_sem=recv_sem,
            device_id=device, device_id_type=MESH,
        )

    def z_copy(k):
        ref = kv.at[z, x, core, y]
        return send(ref, sent.at[k], zr.at[k], device_at(x, y, (z + 8 - unit_step(k)) % 8, core))

    def line_do(i, k, n, act):
        b = (b_pos + SIDE[n]) % 4
        device = device_at(x, y, (z + (7, 1)[i]) % 8, core)

        @pl.when(first)
        def _():
            act(send(kv.at[unit_z(k), :, core, b], sent.at[7], pr.at[i, n], device))

        @pl.when(jnp.logical_not(first))
        def _():
            act(send(kv.at[unit_z(k), b, core], sent.at[7], pr.at[i, n], device))

    def line_send(n):
        for i in range(2):
            line_do(i, 0, n, lambda c: c.start())

    def z_wait(k):
        send(piece(k, 0, 0), sent.at[k], zr.at[k], sibling).wait_recv()

    def one_sent(k):
        return sent.at[jnp.where(k == 0, 6, k)]

    def one_copy(k, slot):
        sign = 1 - 2 * (k % 2)
        if slot == 2:
            return send(piece(k, 4 - sign, 0), one_sent(k), r1.at[k, 2], plane_device(4 + sign, 0))
        return send(piece(k, 0, 0), one_sent(k), r1.at[k, slot], plane_device((1, 3)[slot], 0))

    def one_wait(k, slot):
        send(piece(k, (3, 1, 2)[slot], 0), one_sent(k), r1.at[k, slot], sibling).wait_recv()

    def two_copy(k, m, slot):
        if slot == 2:
            sign = (1, 3)[m % 2]
            return send(piece(k, SIDE[m], 4 - sign), sent.at[k], r2.at[k, m, 2], plane_device(0, sign))
        return send(piece(k, SIDE[m], 0), sent.at[k], r2.at[k, m, slot], plane_device(0, (1, 3)[slot]))

    def two_wait(k, m, slot):
        send(piece(k, SIDE[m], (3, 1, 2)[slot]), sent.at[k], r2.at[k, m, slot], sibling).wait_recv()

    def pair_copy(k, mine):
        ref = kv.at[unit_z(k), :, core if mine else 1 - core]
        return send(ref, sent.at[8], sr.at[k], sibling)

    for c in range(2):
        kv[z, x, core, y, c, 0] = k_ref[c]
        kv[z, x, core, y, c, 1] = v_ref[c]
    barrier = pltpu.get_barrier_semaphore()
    partners = [sibling, plane_device(1, 0), plane_device(3, 0), plane_device(0, 1), plane_device(0, 3)]
    partners += [device_at(x, y, (z + d) % 8, core) for d in range(1, 8)]
    for device in partners:
        pl.semaphore_signal(barrier, inc=1, device_id=device, device_id_type=MESH)
    lane = lax.broadcasted_iota(jnp.int32, (R, 128), 1)
    for c in range(2):
        qv = q_ref[c] * jnp.asarray(0.125, BF)
        zero = jnp.zeros_like(qv)
        qm[c, :R] = jnp.where(lane < 64, qv, zero)
        qm[c, R:] = jnp.where(lane < 64, zero, qv)
    top[...] = jnp.full_like(top, NEG)
    acc[...] = jnp.zeros_like(acc)
    tot[...] = jnp.zeros_like(tot)

    pl.semaphore_wait(barrier, len(partners))

    def first_send(k):
        one_copy(k, 0).start()
        one_copy(k, 1).start()

    def first_send_after(k):
        z_wait(k)
        first_send(k)

    def first_pass(k):
        one_wait(k, 0)
        one_wait(k, 1)
        one_copy(k, 2).start()

    def second_send(k, m):
        two_copy(k, m, 0).start()
        two_copy(k, m, 1).start()

    def second_sends(k):
        for m in range(3):
            second_send(k, m)
        one_wait(k, 2)
        second_send(k, 3)

    def second_pass(k, m):
        two_wait(k, m, 0)
        two_wait(k, m, 1)
        two_copy(k, m, 2).start()

    def pair_send(k):
        for m in range(4):
            two_wait(k, m, 2)
        pair_copy(k, True).start()

    def pair_send_after(i):
        for n in range(4):
            line_do(i, 6 + i, n, lambda c: c.wait_recv())
        pair_copy(6 + i, True).start()

    def ready(k):
        pair_copy(k, False).wait_recv()

    def keys_of(zz, xx, c):
        return (
            kv[zz, xx, :, :, c, 0].reshape(CH, 128),
            kv[zz, xx, :, :, c, 1].reshape(CH, 128),
        )

    mine = core * 8 + inner

    def step_of(k, h):
        zz, xx = unit_z(k), (x + 1 + h) % 4
        c = jnp.where((zz * 4 + xx) % 16 > (z * 4 + x) % 16, 1, 0)
        n = 4 * k + h
        return zz, xx, ((2 * n, 2, 1, 0), (2 * n + 1, c, c, c))

    def edge_masks(zz):
        key = lax.broadcasted_iota(jnp.int32, (CH, 2 * R), 0)
        tok = (lax.broadcasted_iota(jnp.int32, (CH, 2 * R), 1) % R) // 4
        blk = (key // 256) * 8 + ((key // 64) % 4) * 2 + zz // 4
        diag = (blk == mine) & (key % 64 <= tok)
        return (blk < mine) | diag, (blk > mine) | diag

    def forward(k, nxt, cur):
        if nxt is not None:
            par = nxt % 2
            zz, xx, parts = step_of(k, nxt)
            heads = [(keys_of(zz, xx, ck)[0], qm[cq], top[st]) for _, st, cq, ck in parts]
        if cur is not None:
            was = cur % 2
            zc, xc, done = step_of(k, cur)
            tails = [(keys_of(zc, xc, ck)[1], bounds[was, i, 0], bounds[was, i, 1], tot[st], acc[st])
                     for i, (_, st, cq, ck) in enumerate(done)]
        new_tops, sums = [], []
        for i in range(2):
            if nxt is not None:
                kb, qq, old = heads[i]
                s = nt(kb, qq)
                if nxt == 3 and i == 1:
                    off_edge = (zz % 4 != z % 4) | (xx != x)
                    s = jnp.where(edge_masks(zz)[0] | off_edge, s, NEG)
                sbuf[par, i] = s
                new_tops.append((old, jnp.maximum(old, jnp.max(s, axis=0, keepdims=True))))
            if cur is not None:
                vb, old, new, total, a = tails[i]
                p = jnp.exp(sbuf[was, i] - new)
                shrink = jnp.exp(old - new)
                total = total * shrink + jnp.sum(p, axis=0, keepdims=True)
                p = p.astype(BF)
                w[done[i][0]] = p
                sums.append((total, a * shrink + tn(vb, p)))
        if nxt is not None:
            for i, (old, new) in enumerate(new_tops):
                bounds[par, i, 0] = old
                bounds[par, i, 1] = new
                top[parts[i][1]] = new
                tops[parts[i][0]] = new
        if cur is not None:
            for i, (total, a) in enumerate(sums):
                tot[done[i][1]] = total
                acc[done[i][1]] = a

    def forward_edge(k):
        @pl.when((k == 0) | (k == 5))
        def _():
            zz = unit_z(k)
            kb, vb = keys_of(zz, x, 1)
            s = jnp.where(edge_masks(zz)[1], nt(kb, qm[1]), NEG)
            old = top[1]
            new = jnp.maximum(old, jnp.max(s, axis=0, keepdims=True))
            p = jnp.exp(s - new)
            shrink = jnp.exp(old - new)
            tot[1] = tot[1] * shrink + jnp.sum(p, axis=0, keepdims=True)
            p = p.astype(BF)
            acc[1] = acc[1] * shrink + tn(vb, p)
            top[1] = new
            w[64 + k // 5] = p
            tops[64 + k // 5] = new

    def gated(fn, k, last, *args):
        @pl.when(k <= last)
        def _():
            fn(k, *args)

    z_copy(1).start()
    z_copy(2).start()
    first_send(0)
    first_pass(0)
    z_copy(3).start()
    z_copy(4).start()
    for m in range(3):
        second_send(0, m)
    first_send_after(1)
    first_send_after(2)
    z_copy(5).start()
    one_wait(0, 2)
    second_send(0, 3)
    line_send(0)
    for m in range(4):
        second_pass(0, m)
    line_send(1)
    line_send(2)
    first_pass(1)
    first_pass(2)
    second_sends(1)
    first_send_after(3)
    pair_send(0)
    line_send(3)

    def half_turn(t, carry):
        g, late = t // 2, t % 2 == 1

        @pl.when(jnp.logical_not(late))
        def _():
            @pl.when(g <= 4)
            def _():
                for m in range(3):
                    second_send(g + 1, m)

            @pl.when(g <= 2)
            def _():
                first_send_after(g + 3)

        @pl.when(late)
        def _():
            @pl.when(g <= 4)
            def _():
                one_wait(g + 1, 2)
                second_send(g + 1, 3)

            @pl.when((g >= 2) & (g <= 6))
            def _():
                pair_send(g - 1)

            @pl.when(g <= 5)
            def _():
                for m in range(4):
                    second_pass(g, m)

            @pl.when(g <= 3)
            def _():
                first_pass(g + 2)

        unit = jnp.int32(-1)
        for when, what in ORDER:
            unit = jnp.where(t == when, what, unit)

        @pl.when(unit >= 0)
        def _():
            ready(unit)
            forward(unit, 0, None)
            forward(unit, 1, 0)
            forward(unit, 2, 1)
            forward(unit, 3, 2)
            forward(unit, None, 3)
            forward_edge(unit)

        for i in range(2):

            @pl.when(t == LINES[i])
            def _():
                pair_send_after(i)

        return carry

    lax.fori_loop(2, 15, half_turn, 0)

    head = lax.broadcasted_iota(jnp.int32, (1, R), 1) % 4
    lam = jnp.where(
        head == 0, lam_ref[0], jnp.where(head == 1, lam_ref[1], jnp.where(head == 2, lam_ref[2], lam_ref[3]))
    )
    gain = jnp.transpose(jnp.broadcast_to(gain_ref[...] * OUT, (R, 128)))
    for c in range(2):
        a, m, total = acc[c], top[c], tot[c]
        if c == 1:
            m2 = top[2]
            mm = jnp.maximum(m, m2)
            e1, e2 = jnp.exp(m - mm), jnp.exp(m2 - mm)
            a = a * e1 + acc[2] * e2
            total = total * e1 + tot[2] * e2
            m = mm
        a = a / total
        outs = [a[:, :R], a[:, R:]]
        lse = m + jnp.log(total)
        top[c] = lse
        if c == 1:
            top[2] = lse
        differ = outs[0] - lam * outs[1]
        inv = lax.rsqrt(jnp.mean(differ * differ, axis=0, keepdims=True) + EPS)
        att_ref[c] = jnp.transpose(gain * differ * inv).astype(BF)
        scaled = jnp.transpose(og_ref[c].astype(F32)) * gain
        dd = inv * scaled - differ * (inv * inv * inv) * jnp.mean(scaled * differ, axis=0, keepdims=True)
        for j in range(2):
            dots[c, :, j * R:j * R + R] = jnp.sum(dd * outs[j], axis=0, keepdims=True)
        back[c] = jnp.transpose(dd).astype(BF)

    grads[...] = jnp.zeros_like(grads)

    def slopes(t, d, p):
        return [(t - d[:, j * R:j * R + R]).astype(BF) * p[:, j * R:j * R + R] for j in range(2)]

    def gradient(kb, pair):
        return jnp.concatenate([tn(kb, pair[0])[:64], tn(kb, pair[1])[64:]], axis=1)

    def backward(nxt, cur, par):
        if nxt is not None:
            zz, xx, parts = step_of(nxt // 4, nxt % 4)
            heads = [(keys_of(zz, xx, ck)[1], back[cq]) for _, _, cq, ck in parts]
        if cur is not None:
            zc, xc, done = step_of(cur // 4, cur % 4)
            tails = [(keys_of(zc, xc, ck)[0], dots[cq], tops[tid], top[st], grads[st]) for tid, st, cq, ck in done]
        sums = []
        for i in range(2):
            if nxt is not None:
                vb, bk = heads[i]
                sbuf[par, i, :, :R] = nt(vb, bk)
            if cur is not None:
                kb, d, bound, lse, g = tails[i]
                pair = slopes(sbuf[1 - par, i, :, :R], d, w[done[i][0]])
                sums.append(g + gradient(kb, pair) * jnp.exp(bound - lse))
        if cur is not None:
            for i, g in enumerate(sums):
                grads[done[i][1]] = g

    def two_steps(n, carry):
        backward(2 * n + 1, 2 * n, 1)
        backward(2 * n + 2, 2 * n + 1, 0)
        return carry

    backward(0, None, 0)
    lax.fori_loop(0, 15, two_steps, 0)
    backward(31, 30, 1)
    backward(None, 31, 0)
    for i, zz in enumerate((z, (z + 4) % 8)):
        kb, vb = keys_of(zz, x, 1)
        pair = slopes(nt(vb, back[1]), dots[1], w[64 + i])
        grads[1] = grads[1] + gradient(kb, pair) * jnp.exp(tops[64 + i] - top[1])
    for c in range(2):
        g1, g2 = grads[c, :, :R], grads[c, :, R:]
        if c == 1:
            g1, g2 = g1 + grads[2, :, :R], g2 + grads[2, :, R:]
        qg_ref[c] = (0.125 * jnp.transpose(jnp.concatenate([g1, -lam * g2], axis=0))).astype(BF)

    def drain(ref, k):
        send(ref, sent.at[k], sent.at[k], sibling).wait_send()

    drain(kv.at[0, 0:3, 0], 0)
    for k in range(1, 6):
        drain(kv.at[0, :, 0], k)
    drain(kv.at[0, 0, 0, 0:3], 6)
    drain(kv.at[0], 7)
    drain(kv.at[0:4], 8)


def body(queries, key_maps, values, lambdas, norm_gain, out_grad):
    V = pl.BlockSpec(memory_space=pltpu.VMEM)
    S = pl.BlockSpec(memory_space=pltpu.SMEM)
    dma = pltpu.SemaphoreType.DMA
    att, qg = pl.pallas_call(
        kernel,
        out_shape=(jax.ShapeDtypeStruct((2, R, 128), BF),) * 2,
        in_specs=[V, V, V, S, V, V],
        out_specs=(V, V),
        scratch_shapes=[
            pltpu.VMEM((8, 4, 2, 4, 2, 2, 64, 128), BF),
            pltpu.VMEM((66, CH, 2 * R), BF),
            pltpu.VMEM((2, 2 * R, 128), BF),
            pltpu.VMEM((3, 1, 2 * R), F32),
            pltpu.VMEM((3, 1, 2 * R), F32),
            pltpu.VMEM((3, 128, 2 * R), F32),
            pltpu.VMEM((66, 1, 2 * R), F32),
            pltpu.VMEM((2, R, 128), BF),
            pltpu.VMEM((2, 1, 2 * R), F32),
            pltpu.VMEM((3, 64, 2 * R), F32),
            pltpu.VMEM((2, 2, CH, 2 * R), F32),
            pltpu.VMEM((2, 2, 2, 1, 2 * R), F32),
            dma((9,)), dma((8,)), dma((2, 4)), dma((6, 3)), dma((6, 4, 3)), dma((8,)),
        ],
        compiler_params=pltpu.CompilerParams(
            collective_id=0, has_side_effects=True, vmem_limit_bytes=62 * 2**20
        ),
        cost_estimate=pl.CostEstimate(flops=13 * 10**9, bytes_accessed=2**21, transcendentals=17 * 10**6),
    )(
        queries.reshape(2, R, 128),
        key_maps.reshape(2, 64, 128),
        values.reshape(2, 64, 128),
        lambdas,
        norm_gain.reshape(1, 128),
        out_grad.reshape(2, R, 128),
    )
    shape = queries.shape
    return att.reshape(shape), qg.reshape(shape)


def solution(mesh):
    wide = P(None, "outer", "inner", None, None, None)
    keys = P(None, "outer", "inner", None, None)
    return jax.shard_map(
        body, mesh=mesh, in_specs=(wide, keys, keys, P(), P(), wide), out_specs=(wide, wide), check_vma=False
    )
```

```python
import math

import jax
import jax.numpy as jnp
from jax import lax
from jax.experimental import pallas as pl
from jax.experimental.pallas import tpu as pltpu
from jax.sharding import PartitionSpec as P

lam_init = 0.8 - 0.6 * math.exp(-3.3)
OUT = 1.0 - lam_init
EPS = 1e-5
NEG = -1e30
F32, BF = jnp.float32, jnp.bfloat16
R = 256
CH = 512
MESH = pl.DeviceIdType.MESH
ORDER = ((4, 0), (6, 1), (8, 2), (10, 3), (11, 6), (12, 4), (14, 7), (15, 5))
LINES = (9, 12)


def nt(a, b):
    return lax.dot_general(a, b, (((1,), (1,)), ((), ())), preferred_element_type=F32)


def tn(a, b):
    return lax.dot_general(a, b, (((0,), (0,)), ((), ())), preferred_element_type=F32)


def device_at(x, y, z, core):
    return (y * 2 + z // 4, ((z % 4) * 4 + x) * 2 + core)


def kernel(
    q_ref, k_ref, v_ref, lam_ref, gain_ref, og_ref, att_ref, qg_ref,
    kv, w, qm, top, tot, acc, tops, back, dots, grads, sbuf, bounds,
    sent, zr, pr, r1, r2, sr,
):
    inner, outer = lax.axis_index("inner"), lax.axis_index("outer")
    y, z = inner // 2, (inner % 2) * 4 + outer // 8
    x, core = (outer // 2) % 4, outer % 2
    first = core == 0
    a_pos, b_pos = jnp.where(first, x, y), jnp.where(first, y, x)

    def place(a, b):
        return jnp.where(first, a, b), jnp.where(first, b, a)

    def plane_device(da, db):
        px, py = place((a_pos + da) % 4, (b_pos + db) % 4)
        return device_at(px, py, z, core)

    sibling = device_at(x, y, z, 1 - core)
    SIDE = (0, 3, 1, 2)

    def unit_step(k):
        half = jnp.where(k >= 6, 1, jnp.where(k >= 4, 3, jnp.where(k == 3, 4, jnp.where(k == 0, 0, 2))))
        ahead = (k == 1) | (k == 4) | (k == 6)
        return jnp.where(ahead, half, 8 - half)

    def unit_z(k):
        return (z + unit_step(k)) % 8

    def piece(k, da, db):
        px, py = place((a_pos + da) % 4, (b_pos + db) % 4)
        return kv.at[unit_z(k), px, core, py]

    def send(ref, send_sem, recv_sem, device):
        return pltpu.make_async_remote_copy(
            src_ref=ref, dst_ref=ref, send_sem=send_sem, recv_sem=recv_sem,
            device_id=device, device_id_type=MESH,
        )

    def z_copy(k):
        ref = kv.at[z, x, core, y]
        return send(ref, sent.at[k], zr.at[k], device_at(x, y, (z + 8 - unit_step(k)) % 8, core))

    def line_do(i, k, n, act):
        b = (b_pos + SIDE[n]) % 4
        device = device_at(x, y, (z + (7, 1)[i]) % 8, core)

        @pl.when(first)
        def _():
            act(send(kv.at[unit_z(k), :, core, b], sent.at[7], pr.at[i, n], device))

        @pl.when(jnp.logical_not(first))
        def _():
            act(send(kv.at[unit_z(k), b, core], sent.at[7], pr.at[i, n], device))

    def line_send(n):
        for i in range(2):
            line_do(i, 0, n, lambda c: c.start())

    def z_wait(k):
        send(piece(k, 0, 0), sent.at[k], zr.at[k], sibling).wait_recv()

    def one_sent(k):
        return sent.at[jnp.where(k == 0, 6, k)]

    def one_copy(k, slot):
        sign = 1 - 2 * (k % 2)
        if slot == 2:
            return send(piece(k, 4 - sign, 0), one_sent(k), r1.at[k, 2], plane_device(4 + sign, 0))
        return send(piece(k, 0, 0), one_sent(k), r1.at[k, slot], plane_device((1, 3)[slot], 0))

    def one_wait(k, slot):
        send(piece(k, (3, 1, 2)[slot], 0), one_sent(k), r1.at[k, slot], sibling).wait_recv()

    def two_copy(k, m, slot):
        if slot == 2:
            sign = (1, 3)[m % 2]
            return send(piece(k, SIDE[m], 4 - sign), sent.at[k], r2.at[k, m, 2], plane_device(0, sign))
        return send(piece(k, SIDE[m], 0), sent.at[k], r2.at[k, m, slot], plane_device(0, (1, 3)[slot]))

    def two_wait(k, m, slot):
        send(piece(k, SIDE[m], (3, 1, 2)[slot]), sent.at[k], r2.at[k, m, slot], sibling).wait_recv()

    def pair_copy(k, mine):
        ref = kv.at[unit_z(k), :, core if mine else 1 - core]
        return send(ref, sent.at[8], sr.at[k], sibling)

    for c in range(2):
        kv[z, x, core, y, c, 0] = k_ref[c]
        kv[z, x, core, y, c, 1] = v_ref[c]
    barrier = pltpu.get_barrier_semaphore()
    partners = [sibling, plane_device(1, 0), plane_device(3, 0), plane_device(0, 1), plane_device(0, 3)]
    partners += [device_at(x, y, (z + d) % 8, core) for d in range(1, 8)]
    for device in partners:
        pl.semaphore_signal(barrier, inc=1, device_id=device, device_id_type=MESH)
    lane = lax.broadcasted_iota(jnp.int32, (R, 128), 1)
    for c in range(2):
        qv = q_ref[c] * jnp.asarray(0.125, BF)
        zero = jnp.zeros_like(qv)
        qm[c, :R] = jnp.where(lane < 64, qv, zero)
        qm[c, R:] = jnp.where(lane < 64, zero, qv)
    top[...] = jnp.full_like(top, NEG)
    acc[...] = jnp.zeros_like(acc)
    tot[...] = jnp.zeros_like(tot)

    pl.semaphore_wait(barrier, len(partners))

    def first_send(k):
        one_copy(k, 0).start()
        one_copy(k, 1).start()

    def first_send_after(k):
        z_wait(k)
        first_send(k)

    def first_pass(k):
        one_wait(k, 0)
        one_wait(k, 1)
        one_copy(k, 2).start()

    def second_send(k, m):
        two_copy(k, m, 0).start()
        two_copy(k, m, 1).start()

    def second_sends(k):
        for m in range(3):
            second_send(k, m)
        one_wait(k, 2)
        second_send(k, 3)

    def second_pass(k, m):
        two_wait(k, m, 0)
        two_wait(k, m, 1)
        two_copy(k, m, 2).start()

    def pair_send(k):
        for m in range(4):
            two_wait(k, m, 2)
        pair_copy(k, True).start()

    def pair_send_after(i):
        for n in range(4):
            line_do(i, 6 + i, n, lambda c: c.wait_recv())
        pair_copy(6 + i, True).start()

    def ready(k):
        pair_copy(k, False).wait_recv()

    def keys_of(zz, xx, c):
        return (
            kv[zz, xx, :, :, c, 0].reshape(CH, 128),
            kv[zz, xx, :, :, c, 1].reshape(CH, 128),
        )

    mine = core * 8 + inner

    def step_of(k, h):
        zz, xx = unit_z(k), (x + 1 + h) % 4
        c = jnp.where((zz * 4 + xx) % 16 > (z * 4 + x) % 16, 1, 0)
        n = 4 * k + h
        return zz, xx, ((2 * n, 2, 1, 0), (2 * n + 1, c, c, c))

    def edge_masks(zz):
        key = lax.broadcasted_iota(jnp.int32, (CH, 2 * R), 0)
        tok = (lax.broadcasted_iota(jnp.int32, (CH, 2 * R), 1) % R) // 4
        blk = (key // 256) * 8 + ((key // 64) % 4) * 2 + zz // 4
        diag = (blk == mine) & (key % 64 <= tok)
        return (blk < mine) | diag, (blk > mine) | diag

    def forward(k, nxt, cur):
        if nxt is not None:
            par = nxt % 2
            zz, xx, parts = step_of(k, nxt)
            heads = [(keys_of(zz, xx, ck)[0], qm[cq], top[st]) for _, st, cq, ck in parts]
        if cur is not None:
            was = cur % 2
            zc, xc, done = step_of(k, cur)
            tails = [(keys_of(zc, xc, ck)[1], bounds[was, i, 0], bounds[was, i, 1], tot[st], acc[st])
                     for i, (_, st, cq, ck) in enumerate(done)]
        new_tops, sums = [], []
        for i in range(2):
            if nxt is not None:
                kb, qq, old = heads[i]
                s = nt(kb, qq)
                if nxt == 3 and i == 1:
                    off_edge = (zz % 4 != z % 4) | (xx != x)
                    s = jnp.where(edge_masks(zz)[0] | off_edge, s, NEG)
                sbuf[par, i] = s
                new_tops.append((old, jnp.maximum(old, jnp.max(s, axis=0, keepdims=True))))
            if cur is not None:
                vb, old, new, total, a = tails[i]
                p = jnp.exp(sbuf[was, i] - new)
                shrink = jnp.exp(old - new)
                total = total * shrink + jnp.sum(p, axis=0, keepdims=True)
                p = p.astype(BF)
                w[done[i][0]] = p
                sums.append((total, a * shrink + tn(vb, p)))
        if nxt is not None:
            for i, (old, new) in enumerate(new_tops):
                bounds[par, i, 0] = old
                bounds[par, i, 1] = new
                top[parts[i][1]] = new
                tops[parts[i][0]] = new
        if cur is not None:
            for i, (total, a) in enumerate(sums):
                tot[done[i][1]] = total
                acc[done[i][1]] = a

    def forward_edge(k):
        @pl.when((k == 0) | (k == 3))
        def _():
            zz = unit_z(k)
            kb, vb = keys_of(zz, x, 1)
            s = jnp.where(edge_masks(zz)[1], nt(kb, qm[1]), NEG)
            old = top[1]
            new = jnp.maximum(old, jnp.max(s, axis=0, keepdims=True))
            p = jnp.exp(s - new)
            shrink = jnp.exp(old - new)
            tot[1] = tot[1] * shrink + jnp.sum(p, axis=0, keepdims=True)
            p = p.astype(BF)
            acc[1] = acc[1] * shrink + tn(vb, p)
            top[1] = new
            w[64 + k // 3] = p
            tops[64 + k // 3] = new

    def gated(fn, k, last, *args):
        @pl.when(k <= last)
        def _():
            fn(k, *args)

    z_copy(1).start()
    z_copy(2).start()
    first_send(0)
    first_pass(0)
    z_copy(3).start()
    z_copy(4).start()
    for m in range(3):
        second_send(0, m)
    first_send_after(1)
    first_send_after(2)
    z_copy(5).start()
    one_wait(0, 2)
    second_send(0, 3)
    line_send(0)
    for m in range(4):
        second_pass(0, m)
    line_send(1)
    line_send(2)
    first_pass(1)
    first_pass(2)
    second_sends(1)
    first_send_after(3)
    pair_send(0)
    line_send(3)

    def half_turn(t, carry):
        g, late = t // 2, t % 2 == 1

        @pl.when(jnp.logical_not(late))
        def _():
            @pl.when(g <= 4)
            def _():
                for m in range(3):
                    second_send(g + 1, m)

            @pl.when(g <= 2)
            def _():
                first_send_after(g + 3)

        @pl.when(late)
        def _():
            @pl.when(g <= 4)
            def _():
                one_wait(g + 1, 2)
                second_send(g + 1, 3)

            @pl.when(g <= 5)
            def _():
                for m in range(4):
                    second_pass(g, m)

            @pl.when(g <= 3)
            def _():
                first_pass(g + 2)

            @pl.when((g >= 2) & (g <= 6))
            def _():
                pair_send(g - 1)

        unit = jnp.int32(-1)
        for when, what in ORDER:
            unit = jnp.where(t == when, what, unit)

        @pl.when(unit >= 0)
        def _():
            ready(unit)
            forward(unit, 0, None)
            forward(unit, 1, 0)
            forward(unit, 2, 1)
            forward(unit, 3, 2)
            forward(unit, None, 3)
            forward_edge(unit)

        for i in range(2):

            @pl.when(t == LINES[i])
            def _():
                pair_send_after(i)

        return carry

    lax.fori_loop(2, 16, half_turn, 0)

    head = lax.broadcasted_iota(jnp.int32, (1, R), 1) % 4
    lam = jnp.where(
        head == 0, lam_ref[0], jnp.where(head == 1, lam_ref[1], jnp.where(head == 2, lam_ref[2], lam_ref[3]))
    )
    gain = jnp.transpose(jnp.broadcast_to(gain_ref[...] * OUT, (R, 128)))
    for c in range(2):
        a, m, total = acc[c], top[c], tot[c]
        if c == 1:
            m2 = top[2]
            mm = jnp.maximum(m, m2)
            e1, e2 = jnp.exp(m - mm), jnp.exp(m2 - mm)
            a = a * e1 + acc[2] * e2
            total = total * e1 + tot[2] * e2
            m = mm
        a = a / total
        outs = [a[:, :R], a[:, R:]]
        lse = m + jnp.log(total)
        top[c] = lse
        if c == 1:
            top[2] = lse
        differ = outs[0] - lam * outs[1]
        inv = lax.rsqrt(jnp.mean(differ * differ, axis=0, keepdims=True) + EPS)
        att_ref[c] = jnp.transpose(gain * differ * inv).astype(BF)
        scaled = jnp.transpose(og_ref[c].astype(F32)) * gain
        dd = inv * scaled - differ * (inv * inv * inv) * jnp.mean(scaled * differ, axis=0, keepdims=True)
        for j in range(2):
            dots[c, :, j * R:j * R + R] = jnp.sum(dd * outs[j], axis=0, keepdims=True)
        back[c] = jnp.transpose(dd).astype(BF)

    grads[...] = jnp.zeros_like(grads)

    def slopes(t, d, p):
        return [(t - d[:, j * R:j * R + R]).astype(BF) * p[:, j * R:j * R + R] for j in range(2)]

    def gradient(kb, pair):
        return jnp.concatenate([tn(kb, pair[0])[:64], tn(kb, pair[1])[64:]], axis=1)

    def backward(nxt, cur, par):
        if nxt is not None:
            zz, xx, parts = step_of(nxt // 4, nxt % 4)
            heads = [(keys_of(zz, xx, ck)[1], back[cq]) for _, _, cq, ck in parts]
        if cur is not None:
            zc, xc, done = step_of(cur // 4, cur % 4)
            tails = [(keys_of(zc, xc, ck)[0], dots[cq], tops[tid], top[st], grads[st]) for tid, st, cq, ck in done]
        sums = []
        for i in range(2):
            if nxt is not None:
                vb, bk = heads[i]
                sbuf[par, i, :, :R] = nt(vb, bk)
            if cur is not None:
                kb, d, bound, lse, g = tails[i]
                pair = slopes(sbuf[1 - par, i, :, :R], d, w[done[i][0]])
                sums.append(g + gradient(kb, pair) * jnp.exp(bound - lse))
        if cur is not None:
            for i, g in enumerate(sums):
                grads[done[i][1]] = g

    def four_steps(n, carry):
        for i in range(4):
            backward(4 * n + i + 1, 4 * n + i, (i + 1) % 2)
        return carry

    backward(0, None, 0)
    lax.fori_loop(0, 7, four_steps, 0)
    for n in range(28, 31):
        backward(n + 1, n, (n + 1) % 2)
    backward(None, 31, 0)
    for i, zz in enumerate((z, (z + 4) % 8)):
        kb, vb = keys_of(zz, x, 1)
        pair = slopes(nt(vb, back[1]), dots[1], w[64 + i])
        grads[1] = grads[1] + gradient(kb, pair) * jnp.exp(tops[64 + i] - top[1])
    for c in range(2):
        g1, g2 = grads[c, :, :R], grads[c, :, R:]
        if c == 1:
            g1, g2 = g1 + grads[2, :, :R], g2 + grads[2, :, R:]
        qg_ref[c] = (0.125 * jnp.transpose(jnp.concatenate([g1, -lam * g2], axis=0))).astype(BF)

    def drain(ref, k):
        send(ref, sent.at[k], sent.at[k], sibling).wait_send()

    drain(kv.at[0, 0:3, 0], 0)
    for k in range(1, 6):
        drain(kv.at[0, :, 0], k)
    drain(kv.at[0, 0, 0, 0:3], 6)
    drain(kv.at[0], 7)
    drain(kv.at[0:4], 8)


def body(queries, key_maps, values, lambdas, norm_gain, out_grad):
    V = pl.BlockSpec(memory_space=pltpu.VMEM)
    S = pl.BlockSpec(memory_space=pltpu.SMEM)
    dma = pltpu.SemaphoreType.DMA
    att, qg = pl.pallas_call(
        kernel,
        out_shape=(jax.ShapeDtypeStruct((2, R, 128), BF),) * 2,
        in_specs=[V, V, V, S, V, V],
        out_specs=(V, V),
        scratch_shapes=[
            pltpu.VMEM((8, 4, 2, 4, 2, 2, 64, 128), BF),
            pltpu.VMEM((66, CH, 2 * R), BF),
            pltpu.VMEM((2, 2 * R, 128), BF),
            pltpu.VMEM((3, 1, 2 * R), F32),
            pltpu.VMEM((3, 1, 2 * R), F32),
            pltpu.VMEM((3, 128, 2 * R), F32),
            pltpu.VMEM((66, 1, 2 * R), F32),
            pltpu.VMEM((2, R, 128), BF),
            pltpu.VMEM((2, 1, 2 * R), F32),
            pltpu.VMEM((3, 64, 2 * R), F32),
            pltpu.VMEM((2, 2, CH, 2 * R), F32),
            pltpu.VMEM((2, 2, 2, 1, 2 * R), F32),
            dma((9,)), dma((8,)), dma((2, 4)), dma((6, 3)), dma((6, 4, 3)), dma((8,)),
        ],
        compiler_params=pltpu.CompilerParams(
            collective_id=0, has_side_effects=True, vmem_limit_bytes=62 * 2**20
        ),
        cost_estimate=pl.CostEstimate(flops=13 * 10**9, bytes_accessed=2**21, transcendentals=17 * 10**6),
    )(
        queries.reshape(2, R, 128),
        key_maps.reshape(2, 64, 128),
        values.reshape(2, 64, 128),
        lambdas,
        norm_gain.reshape(1, 128),
        out_grad.reshape(2, R, 128),
    )
    shape = queries.shape
    return att.reshape(shape), qg.reshape(shape)


def solution(mesh):
    wide = P(None, "outer", "inner", None, None, None)
    keys = P(None, "outer", "inner", None, None)
    return jax.shard_map(
        body, mesh=mesh, in_specs=(wide, keys, keys, P(), P(), wide), out_specs=(wide, wide), check_vma=False
    )
```

```python
import math

import jax
import jax.numpy as jnp
from jax import lax
from jax.experimental import pallas as pl
from jax.experimental.pallas import tpu as pltpu
from jax.sharding import PartitionSpec as P

lam_init = 0.8 - 0.6 * math.exp(-3.3)
OUT = 1.0 - lam_init
EPS = 1e-5
NEG = -1e30
F32, BF = jnp.float32, jnp.bfloat16
R = 256
CH = 512
MESH = pl.DeviceIdType.MESH
ORDER = ((4, 0), (6, 1), (8, 2), (10, 3), (11, 6), (12, 4), (14, 7), (15, 5))
LINES = (9, 12)


def nt(a, b):
    return lax.dot_general(a, b, (((1,), (1,)), ((), ())), preferred_element_type=F32)


def tn(a, b):
    return lax.dot_general(a, b, (((0,), (0,)), ((), ())), preferred_element_type=F32)


def device_at(x, y, z, core):
    return (y * 2 + z // 4, ((z % 4) * 4 + x) * 2 + core)


def kernel(
    q_ref, k_ref, v_ref, lam_ref, gain_ref, og_ref, att_ref, qg_ref,
    kv, w, qm, top, tot, acc, tops, back, dots, grads, sbuf, bounds,
    sent, zr, pr, r1, r2, sr,
):
    inner, outer = lax.axis_index("inner"), lax.axis_index("outer")
    y, z = inner // 2, (inner % 2) * 4 + outer // 8
    x, core = (outer // 2) % 4, outer % 2
    first = core == 0
    a_pos, b_pos = jnp.where(first, x, y), jnp.where(first, y, x)

    def place(a, b):
        return jnp.where(first, a, b), jnp.where(first, b, a)

    def plane_device(da, db):
        px, py = place((a_pos + da) % 4, (b_pos + db) % 4)
        return device_at(px, py, z, core)

    sibling = device_at(x, y, z, 1 - core)
    SIDE = (0, 3, 1, 2)

    def unit_step(k):
        half = jnp.where(k >= 6, 1, jnp.where(k >= 4, 3, jnp.where(k == 3, 4, jnp.where(k == 0, 0, 2))))
        ahead = (k == 1) | (k == 4) | (k == 6)
        return jnp.where(ahead, half, 8 - half)

    def unit_z(k):
        return (z + unit_step(k)) % 8

    def piece(k, da, db):
        px, py = place((a_pos + da) % 4, (b_pos + db) % 4)
        return kv.at[unit_z(k), px, core, py]

    def send(ref, send_sem, recv_sem, device):
        return pltpu.make_async_remote_copy(
            src_ref=ref, dst_ref=ref, send_sem=send_sem, recv_sem=recv_sem,
            device_id=device, device_id_type=MESH,
        )

    def z_copy(k):
        ref = kv.at[z, x, core, y]
        return send(ref, sent.at[k], zr.at[k], device_at(x, y, (z + 8 - unit_step(k)) % 8, core))

    def line_do(i, k, n, act):
        b = (b_pos + SIDE[n]) % 4
        device = device_at(x, y, (z + (7, 1)[i]) % 8, core)

        @pl.when(first)
        def _():
            act(send(kv.at[unit_z(k), :, core, b], sent.at[7], pr.at[i, n], device))

        @pl.when(jnp.logical_not(first))
        def _():
            act(send(kv.at[unit_z(k), b, core], sent.at[7], pr.at[i, n], device))

    def line_send(n):
        for i in range(2):
            line_do(i, 0, n, lambda c: c.start())

    def z_wait(k):
        send(piece(k, 0, 0), sent.at[k], zr.at[k], sibling).wait_recv()

    def one_sent(k):
        return sent.at[jnp.where(k == 0, 6, k)]

    def one_copy(k, slot):
        sign = 1 - 2 * (k % 2)
        if slot == 2:
            return send(piece(k, 4 - sign, 0), one_sent(k), r1.at[k, 2], plane_device(4 + sign, 0))
        return send(piece(k, 0, 0), one_sent(k), r1.at[k, slot], plane_device((1, 3)[slot], 0))

    def one_wait(k, slot):
        send(piece(k, (3, 1, 2)[slot], 0), one_sent(k), r1.at[k, slot], sibling).wait_recv()

    def two_copy(k, m, slot):
        if slot == 2:
            sign = (1, 3)[m % 2]
            return send(piece(k, SIDE[m], 4 - sign), sent.at[k], r2.at[k, m, 2], plane_device(0, sign))
        return send(piece(k, SIDE[m], 0), sent.at[k], r2.at[k, m, slot], plane_device(0, (1, 3)[slot]))

    def two_wait(k, m, slot):
        send(piece(k, SIDE[m], (3, 1, 2)[slot]), sent.at[k], r2.at[k, m, slot], sibling).wait_recv()

    def pair_copy(k, mine):
        ref = kv.at[unit_z(k), :, core if mine else 1 - core]
        return send(ref, sent.at[8], sr.at[k], sibling)

    for c in range(2):
        kv[z, x, core, y, c, 0] = k_ref[c]
        kv[z, x, core, y, c, 1] = v_ref[c]
    barrier = pltpu.get_barrier_semaphore()
    partners = [sibling, plane_device(1, 0), plane_device(3, 0), plane_device(0, 1), plane_device(0, 3)]
    partners += [device_at(x, y, (z + d) % 8, core) for d in range(1, 8)]
    for device in partners:
        pl.semaphore_signal(barrier, inc=1, device_id=device, device_id_type=MESH)
    lane = lax.broadcasted_iota(jnp.int32, (R, 128), 1)
    for c in range(2):
        qv = q_ref[c] * jnp.asarray(0.125, BF)
        zero = jnp.zeros_like(qv)
        qm[c, :R] = jnp.where(lane < 64, qv, zero)
        qm[c, R:] = jnp.where(lane < 64, zero, qv)
    top[...] = jnp.full_like(top, NEG)
    acc[...] = jnp.zeros_like(acc)
    tot[...] = jnp.zeros_like(tot)

    pl.semaphore_wait(barrier, len(partners))

    def first_send(k):
        one_copy(k, 0).start()
        one_copy(k, 1).start()

    def first_send_after(k):
        z_wait(k)
        first_send(k)

    def first_pass(k):
        one_wait(k, 0)
        one_wait(k, 1)
        one_copy(k, 2).start()

    def second_send(k, m):
        two_copy(k, m, 0).start()
        two_copy(k, m, 1).start()

    def second_sends(k):
        for m in range(3):
            second_send(k, m)
        one_wait(k, 2)
        second_send(k, 3)

    def second_pass(k, m):
        two_wait(k, m, 0)
        two_wait(k, m, 1)
        two_copy(k, m, 2).start()

    def pair_send(k):
        for m in range(4):
            two_wait(k, m, 2)
        pair_copy(k, True).start()

    def pair_send_after(i):
        for n in range(4):
            line_do(i, 6 + i, n, lambda c: c.wait_recv())
        pair_copy(6 + i, True).start()

    def ready(k):
        pair_copy(k, False).wait_recv()

    def keys_of(zz, xx, c):
        return (
            kv[zz, xx, :, :, c, 0].reshape(CH, 128),
            kv[zz, xx, :, :, c, 1].reshape(CH, 128),
        )

    mine = core * 8 + inner

    def step_of(k, h):
        zz, xx = unit_z(k), (x + 1 + h) % 4
        c = jnp.where((zz * 4 + xx) % 16 > (z * 4 + x) % 16, 1, 0)
        n = 4 * k + h
        return zz, xx, ((2 * n, 2, 1, 0), (2 * n + 1, c, c, c))

    def edge_masks(zz):
        key = lax.broadcasted_iota(jnp.int32, (CH, 2 * R), 0)
        tok = (lax.broadcasted_iota(jnp.int32, (CH, 2 * R), 1) % R) // 4
        blk = (key // 256) * 8 + ((key // 64) % 4) * 2 + zz // 4
        diag = (blk == mine) & (key % 64 <= tok)
        return (blk < mine) | diag, (blk > mine) | diag

    def forward(k, nxt, cur):
        if nxt is not None:
            par = nxt % 2
            zz, xx, parts = step_of(k, nxt)
            heads = [(keys_of(zz, xx, ck)[0], qm[cq], top[st]) for _, st, cq, ck in parts]
        if cur is not None:
            was = cur % 2
            zc, xc, done = step_of(k, cur)
            tails = [(keys_of(zc, xc, ck)[1], bounds[was, i, 0], bounds[was, i, 1], tot[st], acc[st])
                     for i, (_, st, cq, ck) in enumerate(done)]
        new_tops, sums = [], []
        for i in range(2):
            if nxt is not None:
                kb, qq, old = heads[i]
                s = nt(kb, qq)
                if nxt == 3 and i == 1:
                    off_edge = (zz % 4 != z % 4) | (xx != x)
                    s = jnp.where(edge_masks(zz)[0] | off_edge, s, NEG)
                sbuf[par, i] = s
                new_tops.append((old, jnp.maximum(old, jnp.max(s, axis=0, keepdims=True))))
            if cur is not None:
                vb, old, new, total, a = tails[i]
                p = jnp.exp(sbuf[was, i] - new)
                shrink = jnp.exp(old - new)
                total = total * shrink + jnp.sum(p, axis=0, keepdims=True)
                p = p.astype(BF)
                w[done[i][0]] = p
                sums.append((total, a * shrink + tn(vb, p)))
        if nxt is not None:
            for i, (old, new) in enumerate(new_tops):
                bounds[par, i, 0] = old
                bounds[par, i, 1] = new
                top[parts[i][1]] = new
                tops[parts[i][0]] = new
        if cur is not None:
            for i, (total, a) in enumerate(sums):
                tot[done[i][1]] = total
                acc[done[i][1]] = a

    def forward_edge(k):
        @pl.when((k == 0) | (k == 3))
        def _():
            zz = unit_z(k)
            kb, vb = keys_of(zz, x, 1)
            s = jnp.where(edge_masks(zz)[1], nt(kb, qm[1]), NEG)
            old = top[1]
            new = jnp.maximum(old, jnp.max(s, axis=0, keepdims=True))
            p = jnp.exp(s - new)
            shrink = jnp.exp(old - new)
            tot[1] = tot[1] * shrink + jnp.sum(p, axis=0, keepdims=True)
            p = p.astype(BF)
            acc[1] = acc[1] * shrink + tn(vb, p)
            top[1] = new
            w[64 + k // 3] = p
            tops[64 + k // 3] = new

    def gated(fn, k, last, *args):
        @pl.when(k <= last)
        def _():
            fn(k, *args)

    z_copy(1).start()
    z_copy(2).start()
    first_send(0)
    first_pass(0)
    z_copy(3).start()
    z_copy(4).start()
    for m in range(3):
        second_send(0, m)
    first_send_after(1)
    first_send_after(2)
    z_copy(5).start()
    one_wait(0, 2)
    second_send(0, 3)
    line_send(0)
    for m in range(4):
        second_pass(0, m)
    line_send(1)
    line_send(2)
    first_pass(1)
    first_pass(2)
    second_sends(1)
    first_send_after(3)
    pair_send(0)
    line_send(3)

    def half_turn(t, carry):
        g, late = t // 2, t % 2 == 1

        @pl.when(jnp.logical_not(late))
        def _():
            @pl.when(g <= 4)
            def _():
                for m in range(3):
                    second_send(g + 1, m)

            @pl.when(g <= 2)
            def _():
                first_send_after(g + 3)

        @pl.when(late)
        def _():
            @pl.when(g <= 4)
            def _():
                one_wait(g + 1, 2)
                second_send(g + 1, 3)

            @pl.when(g <= 5)
            def _():
                for m in range(4):
                    second_pass(g, m)

            @pl.when(g <= 3)
            def _():
                first_pass(g + 2)

            @pl.when((g >= 2) & (g <= 6))
            def _():
                pair_send(g - 1)

        unit = jnp.int32(-1)
        for when, what in ORDER:
            unit = jnp.where(t == when, what, unit)

        @pl.when(unit >= 0)
        def _():
            ready(unit)
            forward(unit, 0, None)
            forward(unit, 1, 0)
            forward(unit, 2, 1)
            forward(unit, 3, 2)
            forward(unit, None, 3)
            forward_edge(unit)

        for i in range(2):

            @pl.when(t == LINES[i])
            def _():
                pair_send_after(i)

        return carry

    lax.fori_loop(2, 16, half_turn, 0)

    head = lax.broadcasted_iota(jnp.int32, (1, R), 1) % 4
    lam = jnp.where(
        head == 0, lam_ref[0], jnp.where(head == 1, lam_ref[1], jnp.where(head == 2, lam_ref[2], lam_ref[3]))
    )
    gain = jnp.transpose(jnp.broadcast_to(gain_ref[...] * OUT, (R, 128)))
    for c in range(2):
        a, m, total = acc[c], top[c], tot[c]
        if c == 1:
            m2 = top[2]
            mm = jnp.maximum(m, m2)
            e1, e2 = jnp.exp(m - mm), jnp.exp(m2 - mm)
            a = a * e1 + acc[2] * e2
            total = total * e1 + tot[2] * e2
            m = mm
        a = a / total
        outs = [a[:, :R], a[:, R:]]
        lse = m + jnp.log(total)
        top[c] = lse
        if c == 1:
            top[2] = lse
        differ = outs[0] - lam * outs[1]
        inv = lax.rsqrt(jnp.mean(differ * differ, axis=0, keepdims=True) + EPS)
        att_ref[c] = jnp.transpose(gain * differ * inv).astype(BF)
        scaled = jnp.transpose(og_ref[c].astype(F32)) * gain
        dd = inv * scaled - differ * (inv * inv * inv) * jnp.mean(scaled * differ, axis=0, keepdims=True)
        for j in range(2):
            dots[c, :, j * R:j * R + R] = jnp.sum(dd * outs[j], axis=0, keepdims=True)
        back[c] = jnp.transpose(dd).astype(BF)

    grads[...] = jnp.zeros_like(grads)

    def slopes(t, d, p):
        return [(t - d[:, j * R:j * R + R]).astype(BF) * p[:, j * R:j * R + R] for j in range(2)]

    def gradient(kb, pair):
        return jnp.concatenate([tn(kb, pair[0])[:64], tn(kb, pair[1])[64:]], axis=1)

    def backward(nxt, cur, par):
        if nxt is not None:
            zz, xx, parts = step_of(nxt // 4, nxt % 4)
            heads = [(keys_of(zz, xx, ck)[1], back[cq]) for _, _, cq, ck in parts]
        if cur is not None:
            zc, xc, done = step_of(cur // 4, cur % 4)
            tails = [(keys_of(zc, xc, ck)[0], dots[cq], tops[tid], top[st], grads[st]) for tid, st, cq, ck in done]
        sums = []
        for i in range(2):
            if nxt is not None:
                vb, bk = heads[i]
                sbuf[par, i, :, :R] = nt(vb, bk)
            if cur is not None:
                kb, d, bound, lse, g = tails[i]
                pair = slopes(sbuf[1 - par, i, :, :R], d, w[done[i][0]])
                sums.append(g + gradient(kb, pair) * jnp.exp(bound - lse))
        if cur is not None:
            for i, g in enumerate(sums):
                grads[done[i][1]] = g

    def eight_steps(n, carry):
        for i in range(8):
            backward(8 * n + i + 1, 8 * n + i, (i + 1) % 2)
        return carry

    backward(0, None, 0)
    lax.fori_loop(0, 3, eight_steps, 0)
    for n in range(24, 31):
        backward(n + 1, n, (n + 1) % 2)
    extra = [keys_of(zz, x, 1) for zz in (z, (z + 4) % 8)]
    through = [nt(vb, back[1]) for _, vb in extra]
    backward(None, 31, 0)
    added = [
        gradient(extra[i][0], slopes(through[i], dots[1], w[64 + i])) * jnp.exp(tops[64 + i] - top[1])
        for i in range(2)
    ]
    grads[1] = grads[1] + added[0] + added[1]
    for c in range(2):
        g1, g2 = grads[c, :, :R], grads[c, :, R:]
        if c == 1:
            g1, g2 = g1 + grads[2, :, :R], g2 + grads[2, :, R:]
        qg_ref[c] = (0.125 * jnp.transpose(jnp.concatenate([g1, -lam * g2], axis=0))).astype(BF)

    def drain(ref, k):
        send(ref, sent.at[k], sent.at[k], sibling).wait_send()

    drain(kv.at[0, 0:3, 0], 0)
    for k in range(1, 6):
        drain(kv.at[0, :, 0], k)
    drain(kv.at[0, 0, 0, 0:3], 6)
    drain(kv.at[0], 7)
    drain(kv.at[0:4], 8)


def body(queries, key_maps, values, lambdas, norm_gain, out_grad):
    V = pl.BlockSpec(memory_space=pltpu.VMEM)
    S = pl.BlockSpec(memory_space=pltpu.SMEM)
    dma = pltpu.SemaphoreType.DMA
    att, qg = pl.pallas_call(
        kernel,
        out_shape=(jax.ShapeDtypeStruct((2, R, 128), BF),) * 2,
        in_specs=[V, V, V, S, V, V],
        out_specs=(V, V),
        scratch_shapes=[
            pltpu.VMEM((8, 4, 2, 4, 2, 2, 64, 128), BF),
            pltpu.VMEM((66, CH, 2 * R), BF),
            pltpu.VMEM((2, 2 * R, 128), BF),
            pltpu.VMEM((3, 1, 2 * R), F32),
            pltpu.VMEM((3, 1, 2 * R), F32),
            pltpu.VMEM((3, 128, 2 * R), F32),
            pltpu.VMEM((66, 1, 2 * R), F32),
            pltpu.VMEM((2, R, 128), BF),
            pltpu.VMEM((2, 1, 2 * R), F32),
            pltpu.VMEM((3, 64, 2 * R), F32),
            pltpu.VMEM((2, 2, CH, 2 * R), F32),
            pltpu.VMEM((2, 2, 2, 1, 2 * R), F32),
            dma((9,)), dma((8,)), dma((2, 4)), dma((6, 3)), dma((6, 4, 3)), dma((8,)),
        ],
        compiler_params=pltpu.CompilerParams(
            collective_id=0, has_side_effects=True, vmem_limit_bytes=62 * 2**20
        ),
        cost_estimate=pl.CostEstimate(flops=13 * 10**9, bytes_accessed=2**21, transcendentals=17 * 10**6),
    )(
        queries.reshape(2, R, 128),
        key_maps.reshape(2, 64, 128),
        values.reshape(2, 64, 128),
        lambdas,
        norm_gain.reshape(1, 128),
        out_grad.reshape(2, R, 128),
    )
    shape = queries.shape
    return att.reshape(shape), qg.reshape(shape)


def solution(mesh):
    wide = P(None, "outer", "inner", None, None, None)
    keys = P(None, "outer", "inner", None, None)
    return jax.shard_map(
        body, mesh=mesh, in_specs=(wide, keys, keys, P(), P(), wide), out_specs=(wide, wide), check_vma=False
    )
```

```python
import math

import jax
import jax.numpy as jnp
from jax import lax
from jax.experimental import pallas as pl
from jax.experimental.pallas import tpu as pltpu
from jax.sharding import PartitionSpec as P

lam_init = 0.8 - 0.6 * math.exp(-3.3)
OUT = 1.0 - lam_init
EPS = 1e-5
NEG = -1e30
F32, BF = jnp.float32, jnp.bfloat16
R = 256
CH = 512
MESH = pl.DeviceIdType.MESH
ORDER = ((4, 0), (6, 1), (8, 2), (10, 3), (11, 6), (12, 4), (14, 7), (15, 5))
LINES = (9, 12)


def nt(a, b):
    return lax.dot_general(a, b, (((1,), (1,)), ((), ())), preferred_element_type=F32)


def tn(a, b):
    return lax.dot_general(a, b, (((0,), (0,)), ((), ())), preferred_element_type=F32)


def device_at(x, y, z, core):
    return (y * 2 + z // 4, ((z % 4) * 4 + x) * 2 + core)


def kernel(
    q_ref, k_ref, v_ref, lam_ref, gain_ref, og_ref, att_ref, qg_ref,
    kv, w, qm, top, tot, acc, tops, back, dots, grads, sbuf, bounds,
    sent, zr, pr, r1, r2, sr,
):
    inner, outer = lax.axis_index("inner"), lax.axis_index("outer")
    y, z = inner // 2, (inner % 2) * 4 + outer // 8
    x, core = (outer // 2) % 4, outer % 2
    first = core == 0
    a_pos, b_pos = jnp.where(first, x, y), jnp.where(first, y, x)

    def place(a, b):
        return jnp.where(first, a, b), jnp.where(first, b, a)

    def plane_device(da, db):
        px, py = place((a_pos + da) % 4, (b_pos + db) % 4)
        return device_at(px, py, z, core)

    sibling = device_at(x, y, z, 1 - core)
    SIDE = (0, 3, 1, 2)

    def unit_step(k):
        half = jnp.where(k >= 6, 1, jnp.where(k >= 4, 3, jnp.where(k == 3, 4, jnp.where(k == 0, 0, 2))))
        ahead = (k == 1) | (k == 4) | (k == 6)
        return jnp.where(ahead, half, 8 - half)

    def unit_z(k):
        return (z + unit_step(k)) % 8

    def piece(k, da, db):
        px, py = place((a_pos + da) % 4, (b_pos + db) % 4)
        return kv.at[unit_z(k), px, core, py]

    def send(ref, send_sem, recv_sem, device):
        return pltpu.make_async_remote_copy(
            src_ref=ref, dst_ref=ref, send_sem=send_sem, recv_sem=recv_sem,
            device_id=device, device_id_type=MESH,
        )

    def z_copy(k):
        ref = kv.at[z, x, core, y]
        return send(ref, sent.at[k], zr.at[k], device_at(x, y, (z + 8 - unit_step(k)) % 8, core))

    def line_do(i, k, n, act):
        b = (b_pos + SIDE[n]) % 4
        device = device_at(x, y, (z + (7, 1)[i]) % 8, core)

        @pl.when(first)
        def _():
            act(send(kv.at[unit_z(k), :, core, b], sent.at[7], pr.at[i, n], device))

        @pl.when(jnp.logical_not(first))
        def _():
            act(send(kv.at[unit_z(k), b, core], sent.at[7], pr.at[i, n], device))

    def line_send(n):
        for i in range(2):
            line_do(i, 0, n, lambda c: c.start())

    def z_wait(k):
        send(piece(k, 0, 0), sent.at[k], zr.at[k], sibling).wait_recv()

    def one_sent(k):
        return sent.at[jnp.where(k == 0, 6, k)]

    def one_copy(k, slot):
        sign = 1 - 2 * (k % 2)
        if slot == 2:
            return send(piece(k, 4 - sign, 0), one_sent(k), r1.at[k, 2], plane_device(4 + sign, 0))
        return send(piece(k, 0, 0), one_sent(k), r1.at[k, slot], plane_device((1, 3)[slot], 0))

    def one_wait(k, slot):
        send(piece(k, (3, 1, 2)[slot], 0), one_sent(k), r1.at[k, slot], sibling).wait_recv()

    def two_copy(k, m, slot):
        if slot == 2:
            sign = (1, 3)[m % 2]
            return send(piece(k, SIDE[m], 4 - sign), sent.at[k], r2.at[k, m, 2], plane_device(0, sign))
        return send(piece(k, SIDE[m], 0), sent.at[k], r2.at[k, m, slot], plane_device(0, (1, 3)[slot]))

    def two_wait(k, m, slot):
        send(piece(k, SIDE[m], (3, 1, 2)[slot]), sent.at[k], r2.at[k, m, slot], sibling).wait_recv()

    def pair_copy(k, mine):
        ref = kv.at[unit_z(k), :, core if mine else 1 - core]
        return send(ref, sent.at[8], sr.at[k], sibling)

    for c in range(2):
        kv[z, x, core, y, c, 0] = k_ref[c]
        kv[z, x, core, y, c, 1] = v_ref[c]
    barrier = pltpu.get_barrier_semaphore()
    partners = [sibling, plane_device(1, 0), plane_device(3, 0), plane_device(0, 1), plane_device(0, 3)]
    partners += [device_at(x, y, (z + d) % 8, core) for d in range(1, 8)]
    for device in partners:
        pl.semaphore_signal(barrier, inc=1, device_id=device, device_id_type=MESH)
    lane = lax.broadcasted_iota(jnp.int32, (R, 128), 1)
    for c in range(2):
        qv = q_ref[c] * jnp.asarray(0.125, BF)
        zero = jnp.zeros_like(qv)
        qm[c, :R] = jnp.where(lane < 64, qv, zero)
        qm[c, R:] = jnp.where(lane < 64, zero, qv)
    top[...] = jnp.full_like(top, NEG)
    acc[...] = jnp.zeros_like(acc)
    tot[...] = jnp.zeros_like(tot)

    pl.semaphore_wait(barrier, len(partners))

    def first_send(k):
        one_copy(k, 0).start()
        one_copy(k, 1).start()

    def first_send_after(k):
        z_wait(k)
        first_send(k)

    def first_pass(k):
        one_wait(k, 0)
        one_wait(k, 1)
        one_copy(k, 2).start()

    def second_send(k, m):
        two_copy(k, m, 0).start()
        two_copy(k, m, 1).start()

    def second_sends(k):
        for m in range(3):
            second_send(k, m)
        one_wait(k, 2)
        second_send(k, 3)

    def second_pass(k, m):
        two_wait(k, m, 0)
        two_wait(k, m, 1)
        two_copy(k, m, 2).start()

    def pair_send(k):
        for m in range(4):
            two_wait(k, m, 2)
        pair_copy(k, True).start()

    def pair_send_after(i):
        for n in range(4):
            line_do(i, 6 + i, n, lambda c: c.wait_recv())
        pair_copy(6 + i, True).start()

    def ready(k):
        pair_copy(k, False).wait_recv()

    def keys_of(zz, xx, c):
        return (
            kv[zz, xx, :, :, c, 0].reshape(CH, 128),
            kv[zz, xx, :, :, c, 1].reshape(CH, 128),
        )

    mine = core * 8 + inner

    def step_of(k, h):
        zz, xx = unit_z(k), (x + 1 + h) % 4
        c = jnp.where((zz * 4 + xx) % 16 > (z * 4 + x) % 16, 1, 0)
        n = 4 * k + h
        return zz, xx, ((2 * n, 2, 1, 0), (2 * n + 1, c, c, c))

    def edge_masks(zz, all_seen):
        key = lax.broadcasted_iota(jnp.int32, (CH, 1), 0)
        tok = (lax.broadcasted_iota(jnp.int32, (1, 2 * R), 1) % R) // 4
        blk = (key // 256) * 8 + ((key // 64) % 4) * 2 + zz // 4
        own = jnp.where(blk == mine, key % 64, 64)
        low = jnp.where((blk < mine) | all_seen, -1, own)
        high = jnp.where(blk > mine, -1, own)
        return low <= tok, high <= tok

    def forward(k, nxt, cur):
        if nxt is not None:
            par = nxt % 2
            zz, xx, parts = step_of(k, nxt)
            heads = [(keys_of(zz, xx, ck)[0], qm[cq], top[st]) for _, st, cq, ck in parts]
        if cur is not None:
            was = cur % 2
            zc, xc, done = step_of(k, cur)
            tails = [(keys_of(zc, xc, ck)[1], bounds[was, i, 0], bounds[was, i, 1], tot[st], acc[st])
                     for i, (_, st, cq, ck) in enumerate(done)]
        new_tops, sums = [], []
        for i in range(2):
            if nxt is not None:
                kb, qq, old = heads[i]
                s = nt(kb, qq)
                if nxt == 3 and i == 1:
                    off_edge = (zz % 4 != z % 4) | (xx != x)
                    s = jnp.where(edge_masks(zz, off_edge)[0], s, NEG)
                sbuf[par, i] = s
                new_tops.append((old, jnp.maximum(old, jnp.max(s, axis=0, keepdims=True))))
            if cur is not None:
                vb, old, new, total, a = tails[i]
                p = jnp.exp(sbuf[was, i] - new)
                shrink = jnp.exp(old - new)
                total = total * shrink + jnp.sum(p, axis=0, keepdims=True)
                p = p.astype(BF)
                w[done[i][0]] = p
                sums.append((total, a * shrink + tn(vb, p)))
        if nxt is not None:
            for i, (old, new) in enumerate(new_tops):
                bounds[par, i, 0] = old
                bounds[par, i, 1] = new
                top[parts[i][1]] = new
                tops[parts[i][0]] = new
        if cur is not None:
            for i, (total, a) in enumerate(sums):
                tot[done[i][1]] = total
                acc[done[i][1]] = a

    def forward_edge(k):
        @pl.when((k == 0) | (k == 3))
        def _():
            zz = unit_z(k)
            kb, vb = keys_of(zz, x, 1)
            s = jnp.where(edge_masks(zz, zz < 0)[1], nt(kb, qm[1]), NEG)
            old = top[1]
            new = jnp.maximum(old, jnp.max(s, axis=0, keepdims=True))
            p = jnp.exp(s - new)
            shrink = jnp.exp(old - new)
            tot[1] = tot[1] * shrink + jnp.sum(p, axis=0, keepdims=True)
            p = p.astype(BF)
            acc[1] = acc[1] * shrink + tn(vb, p)
            top[1] = new
            w[64 + k // 3] = p
            tops[64 + k // 3] = new

    def gated(fn, k, last, *args):
        @pl.when(k <= last)
        def _():
            fn(k, *args)

    z_copy(1).start()
    z_copy(2).start()
    first_send(0)
    first_pass(0)
    z_copy(3).start()
    z_copy(4).start()
    for m in range(3):
        second_send(0, m)
    first_send_after(1)
    first_send_after(2)
    z_copy(5).start()
    one_wait(0, 2)
    second_send(0, 3)
    line_send(0)
    for m in range(4):
        second_pass(0, m)
    line_send(1)
    line_send(2)
    first_pass(1)
    first_pass(2)
    second_sends(1)
    first_send_after(3)
    pair_send(0)
    line_send(3)

    def half_turn(t, carry):
        g, late = t // 2, t % 2 == 1

        @pl.when(jnp.logical_not(late))
        def _():
            @pl.when(g <= 4)
            def _():
                for m in range(3):
                    second_send(g + 1, m)

            @pl.when(g <= 2)
            def _():
                first_send_after(g + 3)

        @pl.when(late)
        def _():
            @pl.when(g <= 4)
            def _():
                one_wait(g + 1, 2)
                second_send(g + 1, 3)

            @pl.when(g <= 5)
            def _():
                for m in range(4):
                    second_pass(g, m)

            @pl.when(g <= 3)
            def _():
                first_pass(g + 2)

            @pl.when((g >= 2) & (g <= 6))
            def _():
                pair_send(g - 1)

        unit = jnp.int32(-1)
        for when, what in ORDER:
            unit = jnp.where(t == when, what, unit)

        @pl.when(unit >= 0)
        def _():
            ready(unit)
            forward(unit, 0, None)
            forward(unit, 1, 0)
            forward(unit, 2, 1)
            forward(unit, 3, 2)
            forward(unit, None, 3)
            forward_edge(unit)

        for i in range(2):

            @pl.when(t == LINES[i])
            def _():
                pair_send_after(i)

        return carry

    lax.fori_loop(2, 16, half_turn, 0)

    head = lax.broadcasted_iota(jnp.int32, (1, R), 1) % 4
    lam = jnp.where(
        head == 0, lam_ref[0], jnp.where(head == 1, lam_ref[1], jnp.where(head == 2, lam_ref[2], lam_ref[3]))
    )
    gain = jnp.transpose(jnp.broadcast_to(gain_ref[...] * OUT, (R, 128)))
    for c in range(2):
        a, m, total = acc[c], top[c], tot[c]
        if c == 1:
            m2 = top[2]
            mm = jnp.maximum(m, m2)
            e1, e2 = jnp.exp(m - mm), jnp.exp(m2 - mm)
            a = a * e1 + acc[2] * e2
            total = total * e1 + tot[2] * e2
            m = mm
        a = a / total
        outs = [a[:, :R], a[:, R:]]
        lse = m + jnp.log(total)
        top[c] = lse
        if c == 1:
            top[2] = lse
        differ = outs[0] - lam * outs[1]
        inv = lax.rsqrt(jnp.mean(differ * differ, axis=0, keepdims=True) + EPS)
        att_ref[c] = jnp.transpose(gain * differ * inv).astype(BF)
        scaled = jnp.transpose(og_ref[c].astype(F32)) * gain
        dd = inv * scaled - differ * (inv * inv * inv) * jnp.mean(scaled * differ, axis=0, keepdims=True)
        for j in range(2):
            dots[c, :, j * R:j * R + R] = jnp.sum(dd * outs[j], axis=0, keepdims=True)
        back[c] = jnp.transpose(dd).astype(BF)

    grads[...] = jnp.zeros_like(grads)

    def slopes(t, d, p):
        return [(t - d[:, j * R:j * R + R]).astype(BF) * p[:, j * R:j * R + R] for j in range(2)]

    def gradient(kb, pair):
        return jnp.concatenate([tn(kb, pair[0])[:64], tn(kb, pair[1])[64:]], axis=1)

    def backward(nxt, cur, par):
        if nxt is not None:
            zz, xx, parts = step_of(nxt // 4, nxt % 4)
            heads = [(keys_of(zz, xx, ck)[1], back[cq]) for _, _, cq, ck in parts]
        if cur is not None:
            zc, xc, done = step_of(cur // 4, cur % 4)
            tails = [(keys_of(zc, xc, ck)[0], dots[cq], tops[tid], top[st], grads[st]) for tid, st, cq, ck in done]
        sums = []
        for i in range(2):
            if nxt is not None:
                vb, bk = heads[i]
                sbuf[par, i, :, :R] = nt(vb, bk)
            if cur is not None:
                kb, d, bound, lse, g = tails[i]
                pair = slopes(sbuf[1 - par, i, :, :R], d, w[done[i][0]])
                sums.append(g + gradient(kb, pair) * jnp.exp(bound - lse))
        if cur is not None:
            for i, g in enumerate(sums):
                grads[done[i][1]] = g

    def eight_steps(n, carry):
        for i in range(8):
            backward(8 * n + i + 1, 8 * n + i, (i + 1) % 2)
        return carry

    backward(0, None, 0)
    lax.fori_loop(0, 3, eight_steps, 0)
    for n in range(24, 31):
        backward(n + 1, n, (n + 1) % 2)
    extra = [keys_of(zz, x, 1) for zz in (z, (z + 4) % 8)]
    through = [nt(vb, back[1]) for _, vb in extra]
    backward(None, 31, 0)
    added = [
        gradient(extra[i][0], slopes(through[i], dots[1], w[64 + i])) * jnp.exp(tops[64 + i] - top[1])
        for i in range(2)
    ]
    grads[1] = grads[1] + added[0] + added[1]
    for c in range(2):
        g1, g2 = grads[c, :, :R], grads[c, :, R:]
        if c == 1:
            g1, g2 = g1 + grads[2, :, :R], g2 + grads[2, :, R:]
        qg_ref[c] = (0.125 * jnp.transpose(jnp.concatenate([g1, -lam * g2], axis=0))).astype(BF)

    def drain(ref, k):
        send(ref, sent.at[k], sent.at[k], sibling).wait_send()

    drain(kv.at[0, 0:3, 0], 0)
    for k in range(1, 6):
        drain(kv.at[0, :, 0], k)
    drain(kv.at[0, 0, 0, 0:3], 6)
    drain(kv.at[0], 7)
    drain(kv.at[0:4], 8)


def body(queries, key_maps, values, lambdas, norm_gain, out_grad):
    V = pl.BlockSpec(memory_space=pltpu.VMEM)
    S = pl.BlockSpec(memory_space=pltpu.SMEM)
    dma = pltpu.SemaphoreType.DMA
    att, qg = pl.pallas_call(
        kernel,
        out_shape=(jax.ShapeDtypeStruct((2, R, 128), BF),) * 2,
        in_specs=[V, V, V, S, V, V],
        out_specs=(V, V),
        scratch_shapes=[
            pltpu.VMEM((8, 4, 2, 4, 2, 2, 64, 128), BF),
            pltpu.VMEM((66, CH, 2 * R), BF),
            pltpu.VMEM((2, 2 * R, 128), BF),
            pltpu.VMEM((3, 1, 2 * R), F32),
            pltpu.VMEM((3, 1, 2 * R), F32),
            pltpu.VMEM((3, 128, 2 * R), F32),
            pltpu.VMEM((66, 1, 2 * R), F32),
            pltpu.VMEM((2, R, 128), BF),
            pltpu.VMEM((2, 1, 2 * R), F32),
            pltpu.VMEM((3, 64, 2 * R), F32),
            pltpu.VMEM((2, 2, CH, 2 * R), F32),
            pltpu.VMEM((2, 2, 2, 1, 2 * R), F32),
            dma((9,)), dma((8,)), dma((2, 4)), dma((6, 3)), dma((6, 4, 3)), dma((8,)),
        ],
        compiler_params=pltpu.CompilerParams(
            collective_id=0, has_side_effects=True, vmem_limit_bytes=62 * 2**20
        ),
        cost_estimate=pl.CostEstimate(flops=13 * 10**9, bytes_accessed=2**21, transcendentals=17 * 10**6),
    )(
        queries.reshape(2, R, 128),
        key_maps.reshape(2, 64, 128),
        values.reshape(2, 64, 128),
        lambdas,
        norm_gain.reshape(1, 128),
        out_grad.reshape(2, R, 128),
    )
    shape = queries.shape
    return att.reshape(shape), qg.reshape(shape)


def solution(mesh):
    wide = P(None, "outer", "inner", None, None, None)
    keys = P(None, "outer", "inner", None, None)
    return jax.shard_map(
        body, mesh=mesh, in_specs=(wide, keys, keys, P(), P(), wide), out_specs=(wide, wide), check_vma=False
    )
```
